512 devices in a mesh: tensor: 16 (over x, y_hi), dp: 32 (over z, y_lo, core).
Axes of the slice: x: 4, y: 8 (y_hi: 4, y_lo: 2; y = y_hi * 2 + y_lo), z: 8, core: 2. Of those that a mesh axis runs over, the one named last changes fastest.
Arguments:
- tokens: bfloat16 [16384, 2048], P(('dp', 'tensor')), parts along dimension 0, may hold values from -6 to 6
- gate_weight: bfloat16 [2048, 6144], P(None, 'tensor'), may hold values from -1 to 1
- up_weight: bfloat16 [2048, 6144], P(None, 'tensor'), may hold values from -1 to 1
- down_weight: bfloat16 [6144, 2048], P('tensor'), may hold values from -1 to 1
- norm_gain: float32 [2048], replicated, may hold values from 0.1 to 1.9
- value_weight: float32 [2048], replicated, may hold values from -0.125 to 0.125
- response_mask: int32 [16384], P('dp'), parts along dimension 0, may hold values from 0 to 1
- sequence_ids: int32 [16384], P('dp'), parts along dimension 0, may hold values from 0 to 15, as said below
Outputs:
- values: float32 [16384], P(('dp', 'tensor')), parts along dimension 0
- mean_values: float32 [512], P('dp'), parts along dimension 0
The draws below stay inside these ranges and needn't reach their ends.
There are 32 independent parts, one for each index of `dp`. The reference program is written for one: setup_inputs(seed, part) draws one part's arguments, and reference() takes and returns one part's arrays. A program takes and returns all parts, laid end to end along the dimension named above; an argument that names none is the same for every part. Nothing has to cross between parts.
Inputs may be any that keep to these rules, and one draw needn't show every extreme that they name: `sequence_ids`: never falls along the tokens; each of the 16 sequences holds at least one token.
All inputs are finite; a program needn't handle non-finite values.
Results may differ from the reference program's by a relative error of at most 0.0011.
Values may be sent and summed in bfloat16 or wider, within the bound.
A program may use at most 64 MiB of HBM per device.

```python
import jax
import jax.numpy as jnp
from jax import lax

D = 2048
FF = 6144
SEQS = 16
TOKENS = 512
N_TENSOR = 16


def split_points(key):
    order = jax.random.permutation(jax.random.fold_in(key, 11), TOKENS - 1) + 1
    flags = jnp.zeros((TOKENS,), jnp.int32).at[order[:SEQS - 1]].set(1)
    return jnp.cumsum(flags).astype(jnp.int32)


def draw_sequence_ids(key, part):
    return split_points(key)


def draw_response_mask(key, part):
    ids = split_points(key)
    key = jax.random.fold_in(key, 5)
    bits = jax.random.randint(key, (TOKENS,), 0, 2)
    dropped = jax.random.randint(jax.random.fold_in(key, 7), (), 0, SEQS)
    return jnp.where(ids == dropped, 0, bits).astype(jnp.int32)


def unit_normal(key, shape):
    return jnp.clip(jax.random.normal(key, shape, jnp.float32), -4.0, 4.0)


def mix_columns(common, own, share, fan_in):
    width = FF // N_TENSOR
    common_weight = jnp.repeat(jnp.sqrt(share), width)[None, :]
    own_weight = jnp.repeat(jnp.sqrt(1.0 - share), width)[None, :]
    return (jnp.tile(common, (1, N_TENSOR)) * common_weight + own * own_weight) / jnp.sqrt(jnp.float32(fan_in))


def draw_gate_weight(key, part):
    key = jax.random.fold_in(key, 21)
    width = FF // N_TENSOR
    common = unit_normal(jax.random.fold_in(key, 1), (D, width))
    own = unit_normal(jax.random.fold_in(key, 2), (D, FF))
    share = jnp.full((N_TENSOR,), 0.6, jnp.float32)
    return mix_columns(common, own, share, D).astype(jnp.bfloat16)


def draw_up_weight(key, part):
    key = jax.random.fold_in(key, 22)
    width = FF // N_TENSOR
    common = unit_normal(jax.random.fold_in(key, 1), (D, width))
    own = unit_normal(jax.random.fold_in(key, 2), (D, FF))
    share = jnp.full((N_TENSOR,), 0.6, jnp.float32)
    return mix_columns(common, own, share, D).astype(jnp.bfloat16)


def draw_down_weight(key, part):
    key = jax.random.fold_in(key, 23)
    width = FF // N_TENSOR
    common = unit_normal(jax.random.fold_in(key, 1), (width, D))
    own = unit_normal(jax.random.fold_in(key, 2), (FF, D))
    share = jnp.full((N_TENSOR,), 0.5, jnp.float32)
    common_weight = jnp.repeat(jnp.sqrt(share), width)[:, None]
    own_weight = jnp.repeat(jnp.sqrt(1.0 - share), width)[:, None]
    return ((jnp.tile(common, (N_TENSOR, 1)) * common_weight + own * own_weight) / jnp.sqrt(jnp.float32(FF))).astype(jnp.bfloat16)


def level_of(stream_key, shape, pieces, smallest, top_value):
    level, own = 1.0, jax.random.fold_in(stream_key, 6)
    for axis_at, shards_of in pieces:
        heights = jnp.exp(jax.random.uniform(jax.random.fold_in(own, axis_at), (shards_of,), jnp.float32, smallest / len(pieces), top_value / len(pieces)))
        level = level * jnp.repeat(heights, shape[axis_at] // shards_of).reshape([-1 if axis == axis_at else 1 for axis in range(len(shape))])
    return level


def normal_values(key, dims, scale, reach, split=(), kind=jnp.bfloat16):
    drawn = jax.random.normal(key, dims, jnp.float32) * scale
    if len(split) > 0:
        drawn = level_of(key, dims, split, -0.22, 0.18) * drawn
    return jnp.clip(drawn, min=-reach, max=reach).astype(kind)


def setup_inputs(seed: int = 0, part: int = 0) -> dict:
    key_list = jax.random.split(jax.random.key(seed), 9)
    part_splits = jax.random.split(jax.random.fold_in(key_list[8], part), 9)
    tokens = normal_values(part_splits[0], (TOKENS, D), 1.0, 6.0, ((0, 16),))
    gate_weight = draw_gate_weight(jax.random.fold_in(key_list[8], 71), part)
    up_weight = draw_up_weight(jax.random.fold_in(key_list[8], 71), part)
    down_weight = draw_down_weight(jax.random.fold_in(key_list[8], 71), part)
    norm_gain = jnp.clip(1.0 + 0.18 * jax.random.normal(key_list[4], (D,), jnp.float32), 0.1, 1.9)
    value_weight = normal_values(key_list[5], (D,), D ** -0.5, 0.125, (), jnp.float32)
    response_mask = draw_response_mask(jax.random.fold_in(jax.random.fold_in(key_list[8], part), 71), part)
    sequence_ids = draw_sequence_ids(jax.random.fold_in(jax.random.fold_in(key_list[8], part), 71), part)
    return {"tokens": tokens, "gate_weight": gate_weight, "up_weight": up_weight, "down_weight": down_weight, "norm_gain": norm_gain, "value_weight": value_weight, "response_mask": response_mask, "sequence_ids": sequence_ids}


def reference(tokens, gate_weight, up_weight, down_weight, norm_gain, value_weight, response_mask, sequence_ids):
    gate = jnp.dot(tokens, gate_weight, preferred_element_type=jnp.float32)
    up = jnp.dot(tokens, up_weight, preferred_element_type=jnp.float32)
    hidden = (jax.nn.silu(gate) * up).astype(jnp.bfloat16)
    total = jnp.dot(hidden, down_weight, preferred_element_type=jnp.float32)
    block = tokens.astype(jnp.float32) + total
    scaled = block * lax.rsqrt(lax.optimization_barrier(jnp.mean(block * block, axis=1, keepdims=True)) + 1e-06)
    values = lax.optimization_barrier(jnp.sum(scaled * norm_gain * value_weight, axis=1))
    onehot = (sequence_ids[:, None] == jnp.arange(SEQS, dtype=jnp.int32)[None, :]).astype(jnp.float32)
    mask_float = response_mask.astype(jnp.float32)
    sums = jnp.dot(mask_float * values, onehot, precision=lax.Precision.HIGHEST)
    counts = jnp.dot(mask_float, onehot, precision=lax.Precision.HIGHEST)
    mean_values = sums / jnp.maximum(counts, 1.0)
    return (values, mean_values)
```

```python
import jax
import jax.numpy as jnp
from jax import lax
from jax.experimental import pallas as pl
from jax.experimental.pallas import tpu as pltpu
from jax.sharding import PartitionSpec as P

SEQS = 16
ROWS = 32
HALF = 16
NX = 4
NY = 4
N = NX * NY
EPS = 1e-06
CHUNK = 512

SPLIT = 1664
COPIES = 104

ORDER = [
"Y:+0 Y:-1 XB:+1 X:0-0",
    "XB:+0 Y:+1 X:0+1 XB:-1",
    "XB:-0 Y:-0 X:0+0 X:0-1",
    "XBF:+ XBF:- YF:+ YF:-",
    "X:1+1 YB:1- X:3+0 X:1-1",
    "YB:0+ YB:3- X:3-0 X:3-1",
    "X:3+1 X:1+0 XF:1- YB:2+",
    "YB:1+ X:2+0 YB:3+ X:2-1",
    "XF:3+ YBF:0 XF:3- YBF:3",
    "YBF:1 X:2-0 YB:2- X:2+1",
    "YBF:2 XF:2+ XF:2- YB:0-",
    "XF:1+ XF:0+ XF:0- X:1-0",
    "GU:3 D:3 S1:3+ S2:3+",
    "S2:3- T1:- S1:3- GU:2",
    "D:2 S2:2- S2:2+ T2:-",
    "T2:+ S1:2+ GU:1 S1:2-",
    "D:1 S2:1+ S2:1- T1:+",
    "SF:2- SF:2+ SF:3- SF:3+",
    "GU:0 TF:+ S1:1+ TF:-",
    "S1:1- SF:1- SF:1+ ZA:2",
    "D:0 S2:0+ S2:0- ZA:3",
    "ZA:1 ZB: S1:0- SF:0+",
    "S1:0+ ZF:1 ZF:3 SF:0-",
    "UF:+ UF:- PX: ZA:0",
]


def kernel(
    tokens, gate_w, up_w, down_w, gain, head, mask, ids,
    result,
    tok, wgu, wd, gain_v, head_v, mask_v, ids_v,
    part, xs, rx2, rxl, rxr, zs, ry2, ryd, ryu, ryb2, rybd, rybu, rxb2, rxbl, rxbr, hidden,
    proj, proj_all, squares, squares_all,
    local_sem, send_sem, recv_sem, p_send, p_recv, s_send, s_recv,
):
    f32, bf16 = jnp.float32, jnp.bfloat16
    me = lax.axis_index("tensor")
    x, y = me // NY, me % NY
    width = tok.shape[2]
    hidden_units = wd.shape[0]

    def at(px, py):
        return lax.rem(px + NX, NX) * NY + lax.rem(py + NY, NY)

    right, left = at(x + 1, y), at(x - 1, y)
    up, down = at(x, y + 1), at(x, y - 1)

    loads = [
        pltpu.make_async_copy(src, dst, local_sem.at[i])
        for i, (src, dst) in enumerate([
            (tokens, tok.at[0, pl.ds(0, ROWS)]),
            (gate_w, wgu.at[:, pl.ds(0, hidden_units)]),
            (up_w, wgu.at[:, pl.ds(hidden_units, hidden_units)]),
            (down_w, wd),
            (gain, gain_v),
            (head, head_v),
            (mask, mask_v),
            (ids, ids_v),
        ])
    ]
    for load in loads:
        load.start()

    barrier = pltpu.get_barrier_semaphore()
    others = [lax.rem(me + k, N) for k in range(1, N)]
    for other in (right, left, up, down):
        pl.semaphore_signal(
            barrier, inc=1, device_id={"tensor": other}, device_id_type=pl.DeviceIdType.MESH
        )
    loads[0].wait()
    pl.semaphore_wait(barrier, 4)

    copies, here, weights = {}, set(), []

    def send(name, src, dst, device):
        number = len(copies)
        copy = pltpu.make_async_remote_copy(
            src_ref=src, dst_ref=dst, send_sem=send_sem.at[number], recv_sem=recv_sem.at[number],
            device_id={"tensor": device}, device_id_type=pl.DeviceIdType.MESH,
        )
        copy.start()
        copies[name] = copy

    def arrived(*names):
        for name in names:
            if name not in here:
                copies[name].wait_recv()
                here.add(name)

    first, second = pl.ds(0, SPLIT), pl.ds(SPLIT, width - SPLIT)
    ring = {"+": (right, up, 3, 0), "-": (left, down, 1, 1)}
    gathered = {dy: set() for dy in range(NY)}

    def rows_of(dx, half):
        return pl.ds(dx * ROWS + half * HALF, HALF)

    def halves(half):
        return pl.ds(half * HALF, HALF)

    y_source = {3: ("Y+0", "Y+1"), 1: ("Y-0", "Y-1"), 2: ("YF+", "YF-")}

    def y_send(d, half):
        src, dst = tok.at[0, rows_of(0, half), first], tok.at[ring[d][2], rows_of(0, half), first]
        send(f"Y{d}{half}", src, dst, ring[d][1])

    def y_forward(d):
        _, to, dy, half = ring[d]
        arrived(f"Y{d}{half}")
        send(f"YF{d}", tok.at[dy, rows_of(0, half), first], tok.at[2, rows_of(0, half), first], to)

    def x_send(dy, d, half):
        if dy:
            arrived(y_source[dy][half])
            gathered[dy].add(y_source[dy][half])
        name = f"X{dy}{d}{half}"
        send(name, tok.at[dy, rows_of(0, half), first], tok.at[dy, rows_of(ring[d][2], half), first], ring[d][0])
        gathered[dy].add(name)

    def x_forward(dy, d):
        to, _, dx, half = ring[d]
        arrived(f"X{dy}{d}{half}")
        send(f"XF{dy}{d}", tok.at[dy, rows_of(dx, half), first], tok.at[dy, rows_of(2, half), first], to)
        gathered[dy].add(f"XF{dy}{d}")

    def xb_send(d, half):
        name = f"XB{d}{half}"
        send(name, tok.at[0, rows_of(0, half), second], tok.at[0, rows_of(ring[d][2], half), second], ring[d][0])
        gathered[0].add(name)

    def xb_forward(d):
        to, _, dx, half = ring[d]
        arrived(f"XB{d}{half}")
        send(f"XBF{d}", tok.at[0, rows_of(dx, half), second], tok.at[0, rows_of(2, half), second], to)
        gathered[0].add(f"XBF{d}")

    def yb_send(dx, d):
        arrived(*{0: (), 3: ("XB+0", "XB+1"), 1: ("XB-0", "XB-1"), 2: ("XBF+", "XBF-")}[dx])
        rows = pl.ds(dx * ROWS, ROWS)
        send(f"YB{dx}{d}", tok.at[0, rows, second], tok.at[ring[d][2], rows, second], ring[d][1])
        gathered[ring[d][2]].add(f"YB{dx}{d}")

    def yb_forward(dx):
        d = "+" if dx % 2 == 0 else "-"
        arrived(f"YB{dx}{d}")
        rows = pl.ds(dx * ROWS, ROWS)
        send(f"YBF{dx}", tok.at[ring[d][2], rows, second], tok.at[2, rows, second], ring[d][1])
        gathered[2].add(f"YBF{dx}")

    lane = lax.broadcasted_iota(jnp.int32, (ROWS, 128), 1)
    row = lax.broadcasted_iota(jnp.int32, (ROWS, 128), 0)
    diagonal = lane % ROWS == row
    tile_lane = lax.broadcasted_iota(jnp.int32, (8, 128), 1) // ROWS
    tile_row = lax.broadcasted_iota(jnp.int32, (8, 128), 0)

    def spread(column, px, py):
        line = jnp.sum(jnp.where(diagonal, column, 0.0), axis=0, keepdims=True)
        return jnp.where((tile_row == px) & (tile_lane == py), line, 0.0)

    def up_project(dy):
        arrived(*sorted(gathered[dy]))
        if not weights:
            for load in loads[1:]:
                load.wait()
            weights.append(gain_v[...] * head_v[...])
        both = jnp.dot(tok[dy], wgu[...], preferred_element_type=f32)
        gate, upper = both[:, :hidden_units], both[:, hidden_units:]
        hidden[dy] = (gate / (1.0 + jnp.exp(-gate)) * upper).astype(bf16)

    def down_project(dy):
        units, gv = hidden[dy], weights[0]
        lanes = jnp.zeros((NX * ROWS, 128), f32)
        for c in range(0, width, CHUNK):
            terms = jnp.dot(units, wd[:, c:c + CHUNK], preferred_element_type=f32)
            part[dy, :, c:c + CHUNK] = terms
            xs[dy, :, c:c + CHUNK] = terms.astype(bf16)
            weighted = terms * gv[:, c:c + CHUNK]
            for k in range(0, CHUNK, 128):
                lanes += weighted[:, k:k + 128]
        column = jnp.sum(lanes, axis=1, keepdims=True)
        total = jnp.zeros((8, 128), f32)
        for dx in range(NX):
            piece = column[dx * ROWS:(dx + 1) * ROWS]
            if dy == 0 and dx == 0:
                piece += jnp.sum(tok[0, :ROWS].astype(f32) * gv, axis=1, keepdims=True)
            total += spread(piece, lax.rem(x + dx, NX), lax.rem(y + dy, NY))
        proj[...] = proj[...] + total

    def x_sum_far(dy, d):
        half = ring[d][3]
        send(f"S2{dy}{d}", xs.at[dy, rows_of(2, half), first], rx2.at[dy, halves(half), first], ring[d][0])

    def x_sum_near(dy, d):
        to, _, back, half = ring[d]
        into = {"+": rxl, "-": rxr}[d]
        send(f"S1{dy}{d}", xs.at[dy, rows_of(4 - back, 1 - half), first], into.at[dy, halves(1 - half), first], to)

    def x_sum_forward(dy, d):
        to, _, back, half = ring[d]
        arrived(f"S2{dy}{d}")
        into = {"+": rxl, "-": rxr}[d]
        rows = rows_of(4 - back, half)
        xs[dy, rows, first] = (part[dy, rows, first] + rx2[dy, halves(half), first].astype(f32)).astype(bf16)
        send(f"SF{dy}{d}", xs.at[dy, rows, first], into.at[dy, halves(half), first], to)

    def x_sum_end(dy):
        arrived(*[f"{kind}{dy}{d}" for kind in ("S1", "SF") for d in "+-"])
        own = pl.ds(0, ROWS)
        total = part[dy, own, first] + rxl[dy, :, first].astype(f32) + rxr[dy, :, first].astype(f32)
        part[dy, own, first] = total
        if dy:
            zs[dy, :, first] = total.astype(bf16)
        if dy == 1:
            send("Z1", zs.at[1, halves(1), first], ryd.at[halves(1), first], up)
        if dy == 3:
            send("Z3", zs.at[3, halves(0), first], ryu.at[halves(0), first], down)
        if dy == 2:
            send("Z2+", zs.at[2, halves(0), first], ry2.at[halves(0), first], up)
            send("Z2-", zs.at[2, halves(1), first], ry2.at[halves(1), first], down)

    def y_sum_forward(dy):
        d, half, into, to = {1: ("+", 0, ryd, up), 3: ("-", 1, ryu, down)}[dy]
        arrived(f"Z2{d}")
        total = part[dy, halves(half), first] + ry2[halves(half), first].astype(f32)
        zs[dy, halves(half), first] = total.astype(bf16)
        send(f"Z{dy}F", zs.at[dy, halves(half), first], into.at[halves(half), first], to)

    lower, upper_half = pl.ds(0, 2 * ROWS), pl.ds(2 * ROWS, 2 * ROWS)

    def yb_sum_far(d):
        rows = {"+": lower, "-": upper_half}[d]
        send(f"T2{d}", xs.at[2, rows, second], ryb2.at[rows], ring[d][1])

    def yb_sum_near(d):
        dy, rows, into = {"+": (1, upper_half, rybd), "-": (3, lower, rybu)}[d]
        send(f"T1{d}", xs.at[dy, rows, second], into.at[rows], ring[d][1])

    def yb_sum_forward(d):
        arrived(f"T2{d}")
        dy, rows, into = {"+": (1, lower, rybd), "-": (3, upper_half, rybu)}[d]
        xs[dy, rows, second] = (part[dy, rows, second] + ryb2[rows].astype(f32)).astype(bf16)
        send(f"TF{d}", xs.at[dy, rows, second], into.at[rows], ring[d][1])

    def yb_sum_end():
        arrived("T1+", "T1-", "TF+", "TF-")
        total = part[0, :, second] + rybd[...].astype(f32) + rybu[...].astype(f32)
        part[0, :, second] = total
        xs[0, :, second] = total.astype(bf16)
        for d in "+-":
            to, _, back, half = ring[d]
            into = {"+": rxbl, "-": rxbr}[d]
            send(f"U2{d}", xs.at[0, rows_of(2, half), second], rxb2.at[halves(half)], to)
            send(f"U1{d}", xs.at[0, rows_of(4 - back, 1 - half), second], into.at[halves(1 - half)], to)

    def xb_sum_forward(d):
        to, _, back, half = ring[d]
        arrived(f"U2{d}")
        into = {"+": rxbl, "-": rxbr}[d]
        rows = rows_of(4 - back, half)
        xs[0, rows, second] = (part[0, rows, second] + rxb2[halves(half)].astype(f32)).astype(bf16)
        send(f"UF{d}", xs.at[0, rows, second], into.at[halves(half)], to)

    def send_projection():
        for k in range(1, N):
            copy = pltpu.make_async_remote_copy(
                src_ref=proj, dst_ref=proj_all.at[N - k], send_sem=p_send.at[k], recv_sem=p_recv.at[N - k],
                device_id={"tensor": others[k - 1]}, device_id_type=pl.DeviceIdType.MESH,
            )
            copy.start()
            p_copies.append(copy)

    proj[...] = jnp.zeros_like(proj)
    p_copies = []
    steps = {
        "Y": lambda k: y_send(k[0], int(k[1])),
        "YF": y_forward,
        "X": lambda k: x_send(int(k[0]), k[1], int(k[2])),
        "XF": lambda k: x_forward(int(k[0]), k[1]),
        "XB": lambda k: xb_send(k[0], int(k[1])),
        "XBF": xb_forward,
        "YB": lambda k: yb_send(int(k[0]), k[1]),
        "YBF": lambda k: yb_forward(int(k)),
        "GU": lambda k: up_project(int(k)),
        "D": lambda k: down_project(int(k)),
        "S2": lambda k: x_sum_far(int(k[0]), k[1]),
        "S1": lambda k: x_sum_near(int(k[0]), k[1]),
        "SF": lambda k: x_sum_forward(int(k[0]), k[1]),
        "ZA": lambda k: x_sum_end(int(k)),
        "ZF": lambda k: y_sum_forward(int(k)),
        "T2": yb_sum_far,
        "T1": yb_sum_near,
        "TF": yb_sum_forward,
        "ZB": lambda k: yb_sum_end(),
        "UF": xb_sum_forward,
        "PX": lambda k: send_projection(),
    }
    for line in ORDER:
        for step in line.split():
            kind, _, key = step.partition(":")
            steps[kind](key)

    mask_f = mask_v[...].astype(f32)
    sequence = lax.broadcasted_iota(jnp.int32, (SEQS, 128), 0)
    chosen = [
        jnp.where(ids_v[r:r + 1, :] == sequence, mask_f[r:r + 1, :], 0.0) for r in range(NX)
    ]
    counts = jnp.sum(chosen[0] + chosen[1] + chosen[2] + chosen[3], axis=1, keepdims=True)

    for copy in p_copies:
        copy.wait_recv()
    all_projected = proj[...]
    for k in range(1, N):
        all_projected += proj_all[k]
    own = pl.ds(0, ROWS)
    begun = tok[0, own, first].astype(f32) + part[0, own, first]
    arrived("Z1", "Z3", "Z1F", "Z3F")
    block = begun + ryd[:, first].astype(f32) + ryu[:, first].astype(f32)
    total = jnp.sum(block * block, axis=1, keepdims=True)
    begun = tok[0, own, second].astype(f32) + part[0, own, second]
    arrived("U1+", "U1-", "UF+", "UF-")
    block = begun + rxbl[...].astype(f32) + rxbr[...].astype(f32)
    total += jnp.sum(block * block, axis=1, keepdims=True)
    squares[...] = spread(total, x, y)
    s_copies = []
    for k in range(1, N):
        copy = pltpu.make_async_remote_copy(
            src_ref=squares, dst_ref=squares_all.at[N - k], send_sem=s_send.at[k], recv_sem=s_recv.at[N - k],
            device_id={"tensor": others[k - 1]}, device_id_type=pl.DeviceIdType.MESH,
        )
        copy.start()
        s_copies.append(copy)

    for copy in copies.values():
        copy.wait_send()
    for copy in p_copies:
        copy.wait_send()
    for copy in s_copies:
        copy.wait_recv()
    all_squares = squares[...]
    for k in range(1, N):
        all_squares += squares_all[k]
    values = all_projected * lax.rsqrt(all_squares / width + EPS)
    sums = chosen[0] * values[0:1]
    for r in range(1, NX):
        sums += chosen[r] * values[r:r + 1]
    means = jnp.sum(sums, axis=1, keepdims=True) / jnp.maximum(counts, 1.0)
    place = lax.broadcasted_iota(jnp.int32, (SEQS, 128), 1)
    row_of_means = jnp.sum(jnp.where(place == sequence + ROWS, means, 0.0), axis=0, keepdims=True)
    mine = jnp.sum(jnp.where(tile_row == x, values, 0.0), axis=0, keepdims=True)
    picked = jnp.zeros((1, ROWS), f32)
    for q in range(NY):
        picked += jnp.where(y == q, mine[:, q * ROWS:(q + 1) * ROWS], 0.0)
    result[...] = row_of_means
    result[:, :ROWS] = picked
    for copy in s_copies:
        copy.wait_send()


def per_device(tokens, gate_w, up_w, down_w, gain, head, mask, ids):
    rows, width = tokens.shape
    units = gate_w.shape[1]
    bf16, f32 = jnp.bfloat16, jnp.float32
    anywhere = pl.BlockSpec(memory_space=pl.ANY)
    result = pl.pallas_call(
        kernel,
        out_shape=jax.ShapeDtypeStruct((1, 128), f32),
        in_specs=[anywhere] * 8,
        out_specs=pl.BlockSpec(memory_space=pltpu.VMEM),
        scratch_shapes=[
            pltpu.VMEM((NY, NX * rows, width), bf16),
            pltpu.VMEM((width, 2 * units), bf16),
            pltpu.VMEM((units, width), bf16),
            pltpu.VMEM((1, width), f32),
            pltpu.VMEM((1, width), f32),
            pltpu.VMEM((NX, 128), jnp.int32),
            pltpu.VMEM((NX, 128), jnp.int32),
            pltpu.VMEM((NY, NX * rows, width), f32),
            pltpu.VMEM((NY, NX * rows, width), bf16),
            pltpu.VMEM((NY, rows, width), bf16),
            pltpu.VMEM((NY, rows, width), bf16),
            pltpu.VMEM((NY, rows, width), bf16),
            pltpu.VMEM((NY, rows, width), bf16),
            pltpu.VMEM((rows, width), bf16),
            pltpu.VMEM((rows, width), bf16),
            pltpu.VMEM((rows, width), bf16),
            pltpu.VMEM((NX * rows, width - SPLIT), bf16),
            pltpu.VMEM((NX * rows, width - SPLIT), bf16),
            pltpu.VMEM((NX * rows, width - SPLIT), bf16),
            pltpu.VMEM((rows, width - SPLIT), bf16),
            pltpu.VMEM((rows, width - SPLIT), bf16),
            pltpu.VMEM((rows, width - SPLIT), bf16),
            pltpu.VMEM((NY, NX * rows, units), bf16),
            pltpu.VMEM((8, 128), f32),
            pltpu.VMEM((N, 8, 128), f32),
            pltpu.VMEM((8, 128), f32),
            pltpu.VMEM((N, 8, 128), f32),
            pltpu.SemaphoreType.DMA((8,)),
            pltpu.SemaphoreType.DMA((COPIES,)),
            pltpu.SemaphoreType.DMA((COPIES,)),
            pltpu.SemaphoreType.DMA((N,)),
            pltpu.SemaphoreType.DMA((N,)),
            pltpu.SemaphoreType.DMA((N,)),
            pltpu.SemaphoreType.DMA((N,)),
        ],
        compiler_params=pltpu.CompilerParams(
            collective_id=0, has_side_effects=True, vmem_limit_bytes=56 * 1024 * 1024
        ),
    )(
        tokens, gate_w, up_w, down_w,
        gain.reshape(1, width), head.reshape(1, width),
        mask.reshape(NX, 128), ids.reshape(NX, 128),
    )
    return result[0, :rows], result[0, rows:rows + SEQS]


def solution(mesh):
    placed = (
        P(("dp", "tensor"), None),
        P(None, "tensor"),
        P(None, "tensor"),
        P("tensor", None),
        P(),
        P(),
        P("dp"),
        P("dp"),
    )
    return jax.shard_map(
        per_device,
        mesh=mesh,
        in_specs=placed,
        out_specs=(P(("dp", "tensor")), P("dp")),
        check_vma=False,
    )
```

```python
import jax
import jax.numpy as jnp
from jax import lax
from jax.experimental import pallas as pl
from jax.experimental.pallas import tpu as pltpu
from jax.sharding import PartitionSpec as P

SEQS = 16
ROWS = 32
HALF = 16
NX = 4
NY = 4
N = NX * NY
EPS = 1e-06
CHUNK = 512

SPLIT = 1664
ARRIVALS = 64

KIND_ROWS = {"X": 384, "S": 384, "Y": 96, "Z": 96, "XB": 96, "YB": 384, "T": 384, "U": 96}
KINDS = tuple(KIND_ROWS)
GROUPS = {f"{letter}{dy}": 64 for letter in "xs" for dy in range(NY)}
GROUPS.update({"z": 64, "b+": 64, "b-": 64, "bf": 128, "t": 256, "u": 64})

SLOT = (0, 1, 3, 2)

ORDER = [
    "Y:-1 Y:+0 X:0+0 XB:-1",
    "X:0-1 XB:+0 Y:-0 X:0+1",
    "Y:+1 XB:-0 X:0-0 XF:0-",
    "XBF:- XB:+1 XBF:+ XF:0+",
    "YF:- YF:+ X:1-1 YB:0+",
    "X:3-0 X:1+1 YB:1- X:3+0",
    "YB:2+ X:1+0 X:3-1 GU:0",
    "YB:3- XF:1- X:3+1 YB:2-",
    "YB:1+ YB:3+ X:2-1 X:2+0",
    "XF:3- YBF:1 XF:3+ X:2+1",
    "YBF:0 X:2-0 D:0 YBF:2",
    "YBF:3 XF:2- XF:2+ X:1-0",
    "YB:0- XF:1+ GU:3 D:3",
    "S2:3+ S1:3+ S1:3- S2:3-",
    "GU:2 D:2 S2:2+ T2:+",
    "S2:2- T2:- S1:2- GU:1",
    "S1:2+ D:1 S2:1- S2:1+",
    "T1:+ T1:- SF:2+ SF:2-",
    "SF:3+ SF:3- TF:+ S1:1-",
    "TF:- SF:1- S2:0- S1:1+",
    "SF:1+ ZA:2 S1:0+ ZA:3",
    "S2:0+ ZA:1 ZB: S1:0-",
    "ZF:1 ZF:3 SF:0+ SF:0-",
    "UF:- UF:+ ZA:0",
]


def kernel(
    tokens, gate_w, up_w, down_w, gain, head, mask, ids,
    result,
    tok, wgu, wd, gain_v, head_v, mask_v, ids_v,
    part, xs, rx2, rxl, rxr, zs, ry2, ryd, ryu, ryb2, rybd, rybu, rxb2, rxbl, rxbr, hidden,
    proj, proj_all, line_out, lines,
    local_sem, send_sem, recv_sem, small_sem,
):
    f32, bf16 = jnp.float32, jnp.bfloat16
    me, dp = lax.axis_index("tensor"), lax.axis_index("dp")
    x, y = me // NY, me % NY
    width = tok.shape[2]
    hidden_units = wd.shape[0]

    places_x = [x] + [lax.rem(x + k, NX) for k in range(1, NX)]
    places_y = [y] + [lax.rem(y + k, NY) for k in range(1, NY)]
    device_at = {(dy, dx): places_x[dx] * NY + places_y[dy] for dy in range(NY) for dx in range(NX)}
    right, left, up, down = device_at[0, 1], device_at[0, 3], device_at[1, 0], device_at[3, 0]

    loads = [
        pltpu.make_async_copy(src, dst, local_sem.at[i])
        for i, (src, dst) in enumerate([
            (tokens, tok.at[0, pl.ds(0, ROWS)]),
            (gate_w, wgu.at[:, pl.ds(0, hidden_units)]),
            (up_w, wgu.at[:, pl.ds(hidden_units, hidden_units)]),
            (down_w, wd),
            (gain, gain_v),
            (head, head_v),
            (mask, mask_v),
            (ids, ids_v),
        ])
    ]
    barrier = pltpu.get_barrier_semaphore()
    for other in (right, left, up, down):
        pl.semaphore_signal(
            barrier, inc=1, device_id=(other, dp), device_id_type=pl.DeviceIdType.MESH
        )
    loads[0].start()
    loads[0].wait()
    pl.semaphore_wait(barrier, 4)

    here, weights = set(), []
    arrivals = {}
    first, second = pl.ds(0, SPLIT), pl.ds(SPLIT, width - SPLIT)

    def sized(rows, columns):
        if rows <= NX * ROWS:
            return tok.at[0, pl.ds(0, rows), columns]
        return tok.at[pl.ds(0, rows // (NX * ROWS)), :, columns]

    def await_bytes(like, sem):
        pltpu.make_async_copy(like, like, sem).wait()

    def send(name, src, dst, device, kind, group=None):
        key = group or name
        if key not in arrivals:
            arrivals[key] = (recv_sem.at[len(arrivals)], dst)
        pltpu.make_async_remote_copy(
            src_ref=src, dst_ref=dst, send_sem=send_sem.at[KINDS.index(kind)], recv_sem=arrivals[key][0],
            device_id=(device, dp), device_id_type=pl.DeviceIdType.MESH,
        ).start()

    def arrived(*names):
        for name in names:
            if name not in here:
                sem, dst = arrivals[name]
                if name in GROUPS:
                    dst = sized(GROUPS[name], first if name[0] in "xsz" else second)
                await_bytes(dst, sem)
                here.add(name)

    ring = {"+": (right, up, 3, 0), "-": (left, down, 1, 1)}
    gathered = {dy: set() for dy in range(NY)}

    def rows_of(dx, half):
        return pl.ds(dx * ROWS + half * HALF, HALF)

    def halves(half):
        return pl.ds(half * HALF, HALF)

    y_source = {3: ("Y+0", "Y+1"), 1: ("Y-0", "Y-1"), 2: ("YF+", "YF-")}

    def y_send(d, half):
        src, dst = tok.at[0, rows_of(0, half), first], tok.at[SLOT[ring[d][2]], rows_of(0, half), first]
        send(f"Y{d}{half}", src, dst, ring[d][1], "Y")

    def y_forward(d):
        _, to, dy, half = ring[d]
        arrived(f"Y{d}{half}")
        send(f"YF{d}", tok.at[SLOT[dy], rows_of(0, half), first], tok.at[SLOT[2], rows_of(0, half), first], to, "Y")

    def x_send(dy, d, half):
        if dy:
            arrived(y_source[dy][half])
            gathered[dy].add(y_source[dy][half])
        to, _, dx, ahead = ring[d]
        group = None if half == ahead else f"x{dy}"
        src, dst = tok.at[SLOT[dy], rows_of(0, half), first], tok.at[SLOT[dy], rows_of(dx, half), first]
        send(f"X{dy}{d}{half}", src, dst, to, "X", group)

    def x_forward(dy, d):
        to, _, dx, half = ring[d]
        arrived(f"X{dy}{d}{half}")
        src, dst = tok.at[SLOT[dy], rows_of(dx, half), first], tok.at[SLOT[dy], rows_of(2, half), first]
        send(f"XF{dy}{d}", src, dst, to, "X", f"x{dy}")
        gathered[dy].add(f"x{dy}")

    def xb_send(d, half):
        name = f"XB{d}{half}"
        send(name, tok.at[0, rows_of(0, half), second], tok.at[0, rows_of(ring[d][2], half), second], ring[d][0], "XB")
        gathered[0].add(name)

    def xb_forward(d):
        to, _, dx, half = ring[d]
        arrived(f"XB{d}{half}")
        send(f"XBF{d}", tok.at[0, rows_of(dx, half), second], tok.at[0, rows_of(2, half), second], to, "XB")
        gathered[0].add(f"XBF{d}")

    def yb_send(dx, d):
        arrived(*{0: (), 3: ("XB+0", "XB+1"), 1: ("XB-0", "XB-1"), 2: ("XBF+", "XBF-")}[dx])
        rows = pl.ds(dx * ROWS, ROWS)
        group = None if (dx % 2 == 0) == (d == "+") else f"b{d}"
        send(f"YB{dx}{d}", tok.at[0, rows, second], tok.at[SLOT[ring[d][2]], rows, second], ring[d][1], "YB", group)
        gathered[ring[d][2]].add(group or f"YB{dx}{d}")

    def yb_forward(dx):
        d = "+" if dx % 2 == 0 else "-"
        arrived(f"YB{dx}{d}")
        rows = pl.ds(dx * ROWS, ROWS)
        send(f"YBF{dx}", tok.at[SLOT[ring[d][2]], rows, second], tok.at[SLOT[2], rows, second], ring[d][1], "YB", "bf")
        gathered[2].add("bf")

    lane = lax.broadcasted_iota(jnp.int32, (ROWS, 128), 1)
    row = lax.broadcasted_iota(jnp.int32, (ROWS, 128), 0)
    diagonal = lane % ROWS == row
    def as_line(column):
        return jnp.sum(jnp.where(diagonal, column, 0.0), axis=0, keepdims=True)

    def small_copy(dy, dx, src, dst, pair):
        pltpu.make_async_remote_copy(
            src_ref=src, dst_ref=dst.at[-dy % NY * NX + -dx % NX],
            send_sem=small_sem.at[pair, 0], recv_sem=small_sem.at[pair, 1],
            device_id=(device_at[dy, dx], dp), device_id_type=pl.DeviceIdType.MESH,
        ).start()

    def up_project(offsets):
        for dy in offsets:
            arrived(*sorted(gathered[dy]))
        if not weights:
            for load in loads[1:]:
                load.wait()
            weights.append(gain_v[...] * head_v[...])
        at_slot = pl.ds(min(SLOT[dy] for dy in offsets), len(offsets))
        rows = len(offsets) * NX * ROWS
        both = jnp.dot(tok[at_slot].reshape(rows, width), wgu[...], preferred_element_type=f32)
        gate, upper = both[:, :hidden_units], both[:, hidden_units:]
        units = (gate / (1.0 + jnp.exp(-gate)) * upper).astype(bf16)
        hidden[at_slot] = units.reshape(len(offsets), NX * ROWS, hidden_units)

    def down_project(offsets):
        at_slot = pl.ds(min(SLOT[dy] for dy in offsets), len(offsets))
        rows = len(offsets) * NX * ROWS
        units, gv = hidden[at_slot].reshape(rows, hidden_units), weights[0]
        lanes = jnp.zeros((rows, 128), f32)
        for c in range(0, width, CHUNK):
            terms = jnp.dot(units, wd[:, c:c + CHUNK], preferred_element_type=f32)
            shaped = terms.reshape(len(offsets), NX * ROWS, CHUNK)
            part[at_slot, :, c:c + CHUNK] = shaped
            xs[at_slot, :, c:c + CHUNK] = shaped.astype(bf16)
            weighted = terms * gv[:, c:c + CHUNK]
            for k in range(0, CHUNK, 128):
                lanes += weighted[:, k:k + 128]
        column = jnp.sum(lanes, axis=1, keepdims=True)
        for place, dy in enumerate(sorted(offsets, key=lambda q: SLOT[q])):
            for dx in range(NX):
                begin = (place * NX + dx) * ROWS
                piece = column[begin:begin + ROWS]
                if dy == 0 and dx == 0:
                    piece += jnp.sum(tok[0, :ROWS].astype(f32) * gv, axis=1, keepdims=True)
                    proj_all[0] = as_line(piece)
                else:
                    proj[dy * NX + dx] = as_line(piece)
            for dx in range(NX):
                if dy or dx:
                    small_copy(dy, dx, proj.at[dy * NX + dx], proj_all, 0)

    def x_sum_far(dy, d):
        half = ring[d][3]
        send(f"S2{dy}{d}", xs.at[SLOT[dy], rows_of(2, half), first], rx2.at[dy, halves(half), first], ring[d][0], "S")

    def x_sum_near(dy, d):
        to, _, back, half = ring[d]
        into = {"+": rxl, "-": rxr}[d]
        src, dst = xs.at[SLOT[dy], rows_of(4 - back, 1 - half), first], into.at[dy, halves(1 - half), first]
        send(f"S1{dy}{d}", src, dst, to, "S", f"s{dy}")

    def x_sum_forward(dy, d):
        to, _, back, half = ring[d]
        arrived(f"S2{dy}{d}")
        into = {"+": rxl, "-": rxr}[d]
        rows = rows_of(4 - back, half)
        xs[SLOT[dy], rows, first] = (part[SLOT[dy], rows, first] + rx2[dy, halves(half), first].astype(f32)).astype(bf16)
        send(f"SF{dy}{d}", xs.at[SLOT[dy], rows, first], into.at[dy, halves(half), first], to, "S", f"s{dy}")

    def x_sum_end(dy):
        arrived(f"s{dy}")
        own = pl.ds(0, ROWS)
        total = part[SLOT[dy], own, first] + rxl[dy, :, first].astype(f32) + rxr[dy, :, first].astype(f32)
        part[SLOT[dy], own, first] = total
        if dy:
            zs[dy, :, first] = total.astype(bf16)
        if dy == 1:
            send("Z1", zs.at[1, halves(1), first], ryd.at[halves(1), first], up, "Z", "z")
        if dy == 3:
            send("Z3", zs.at[3, halves(0), first], ryu.at[halves(0), first], down, "Z", "z")
        if dy == 2:
            send("Z2+", zs.at[2, halves(0), first], ry2.at[halves(0), first], up, "Z")
            send("Z2-", zs.at[2, halves(1), first], ry2.at[halves(1), first], down, "Z")

    def y_sum_forward(dy):
        d, half, into, to = {1: ("+", 0, ryd, up), 3: ("-", 1, ryu, down)}[dy]
        arrived(f"Z2{d}")
        total = part[SLOT[dy], halves(half), first] + ry2[halves(half), first].astype(f32)
        zs[dy, halves(half), first] = total.astype(bf16)
        send(f"Z{dy}F", zs.at[dy, halves(half), first], into.at[halves(half), first], to, "Z", "z")

    lower, upper_half = pl.ds(0, 2 * ROWS), pl.ds(2 * ROWS, 2 * ROWS)

    def yb_sum_far(d):
        rows = {"+": lower, "-": upper_half}[d]
        send(f"T2{d}", xs.at[SLOT[2], rows, second], ryb2.at[rows], ring[d][1], "T")

    def yb_sum_near(d):
        dy, rows, into = {"+": (1, upper_half, rybd), "-": (3, lower, rybu)}[d]
        send(f"T1{d}", xs.at[SLOT[dy], rows, second], into.at[rows], ring[d][1], "T", "t")

    def yb_sum_forward(d):
        arrived(f"T2{d}")
        dy, rows, into = {"+": (1, lower, rybd), "-": (3, upper_half, rybu)}[d]
        xs[SLOT[dy], rows, second] = (part[SLOT[dy], rows, second] + ryb2[rows].astype(f32)).astype(bf16)
        send(f"TF{d}", xs.at[SLOT[dy], rows, second], into.at[rows], ring[d][1], "T", "t")

    def yb_sum_end():
        arrived("t")
        total = part[0, :, second] + rybd[...].astype(f32) + rybu[...].astype(f32)
        part[0, :, second] = total
        xs[0, :, second] = total.astype(bf16)
        for d in "+-":
            to, _, back, half = ring[d]
            into = {"+": rxbl, "-": rxbr}[d]
            send(f"U2{d}", xs.at[0, rows_of(2, half), second], rxb2.at[halves(half)], to, "U")
            send(f"U1{d}", xs.at[0, rows_of(4 - back, 1 - half), second], into.at[halves(1 - half)], to, "U", "u")

    def xb_sum_forward(d):
        to, _, back, half = ring[d]
        arrived(f"U2{d}")
        into = {"+": rxbl, "-": rxbr}[d]
        rows = rows_of(4 - back, half)
        xs[0, rows, second] = (part[0, rows, second] + rxb2[halves(half)].astype(f32)).astype(bf16)
        send(f"UF{d}", xs.at[0, rows, second], into.at[halves(half)], to, "U", "u")

    steps = {
        "Y": lambda k: y_send(k[0], int(k[1])),
        "YF": y_forward,
        "X": lambda k: x_send(int(k[0]), k[1], int(k[2])),
        "XF": lambda k: x_forward(int(k[0]), k[1]),
        "XB": lambda k: xb_send(k[0], int(k[1])),
        "XBF": xb_forward,
        "YB": lambda k: yb_send(int(k[0]), k[1]),
        "YBF": lambda k: yb_forward(int(k)),
        "GU": lambda k: up_project([int(q) for q in k]),
        "D": lambda k: down_project([int(q) for q in k]),
        "S2": lambda k: x_sum_far(int(k[0]), k[1]),
        "S1": lambda k: x_sum_near(int(k[0]), k[1]),
        "SF": lambda k: x_sum_forward(int(k[0]), k[1]),
        "ZA": lambda k: x_sum_end(int(k)),
        "ZF": lambda k: y_sum_forward(int(k)),
        "T2": yb_sum_far,
        "T1": yb_sum_near,
        "TF": yb_sum_forward,
        "ZB": lambda k: yb_sum_end(),
        "UF": xb_sum_forward,
    }
    for number, line in enumerate(ORDER):
        if number == 2:
            for load in loads[1:]:
                load.start()
        for step in line.split():
            kind, _, key = step.partition(":")
            steps[kind](key)

    mask_f = mask_v[...].astype(f32)
    sequence = lax.broadcasted_iota(jnp.int32, (SEQS, 128), 0)
    chosen = [
        jnp.where(ids_v[r:r + 1, :] == sequence, mask_f[r:r + 1, :], 0.0) for r in range(NX)
    ]
    counts = jnp.sum(chosen[0] + chosen[1] + chosen[2] + chosen[3], axis=1, keepdims=True)

    others = pl.ds(1, N - 1)
    await_bytes(proj_all.at[others], small_sem.at[0, 1])
    projected = jnp.sum(proj_all[...], axis=0)
    own = pl.ds(0, ROWS)
    begun = tok[0, own, first].astype(f32) + part[0, own, first]
    arrived("z")
    block = begun + ryd[:, first].astype(f32) + ryu[:, first].astype(f32)
    total = jnp.sum(block * block, axis=1, keepdims=True)
    begun = tok[0, own, second].astype(f32) + part[0, own, second]
    arrived("u")
    block = begun + rxbl[...].astype(f32) + rxbr[...].astype(f32)
    total += jnp.sum(block * block, axis=1, keepdims=True)
    line = projected * lax.rsqrt(as_line(total) / width + EPS)
    mine = jnp.where(lax.broadcasted_iota(jnp.int32, (1, 128), 1) // ROWS == y, line, 0.0)
    line_out[...] = mine
    lines[0] = mine
    far_first = sorted(
        ((dy, dx) for dy in range(NY) for dx in range(NX) if dy or dx),
        key=lambda q: -2 * min(q[0], NY - q[0]) - min(q[1], NX - q[1]),
    )
    for dy, dx in far_first:
        small_copy(dy, dx, line_out, lines, 1)
    for kind, rows in KIND_ROWS.items():
        await_bytes(sized(rows, first if kind in ("X", "S", "Y", "Z") else second), send_sem.at[KINDS.index(kind)])
    await_bytes(proj.at[others], small_sem.at[0, 0])
    await_bytes(lines.at[others], small_sem.at[1, 1])
    tile_row = lax.broadcasted_iota(jnp.int32, (8, 128), 0)
    values = jnp.zeros((8, 128), f32)
    for dx in range(NX):
        column = lines[dx] + lines[NX + dx] + lines[2 * NX + dx] + lines[3 * NX + dx]
        values += jnp.where(tile_row == places_x[dx], column, 0.0)
    sums = chosen[0] * values[0:1]
    for r in range(1, NX):
        sums += chosen[r] * values[r:r + 1]
    means = jnp.sum(sums, axis=1, keepdims=True) / jnp.maximum(counts, 1.0)
    place = lax.broadcasted_iota(jnp.int32, (SEQS, 128), 1)
    result[...] = jnp.sum(jnp.where(place == sequence + ROWS, means, 0.0), axis=0, keepdims=True)
    result[:, :ROWS] = line[:, :ROWS]
    await_bytes(lines.at[others], small_sem.at[1, 0])


def take_apart(row, values_out, means_out):
    values_out[...] = row[:, :ROWS]
    means_out[...] = row[:, ROWS:ROWS + SEQS]


def per_device(tokens, gate_w, up_w, down_w, gain, head, mask, ids):
    rows, width = tokens.shape
    units = gate_w.shape[1]
    bf16, f32 = jnp.bfloat16, jnp.float32
    anywhere = pl.BlockSpec(memory_space=pl.ANY)
    result = pl.pallas_call(
        kernel,
        out_shape=pltpu.VMEM((1, 128), f32),
        in_specs=[anywhere] * 8,
        out_specs=pl.BlockSpec(memory_space=pltpu.VMEM),
        scratch_shapes=[
            pltpu.VMEM((NY, NX * rows, width), bf16),
            pltpu.VMEM((width, 2 * units), bf16),
            pltpu.VMEM((units, width), bf16),
            pltpu.VMEM((1, width), f32),
            pltpu.VMEM((1, width), f32),
            pltpu.VMEM((NX, 128), jnp.int32),
            pltpu.VMEM((NX, 128), jnp.int32),
            pltpu.VMEM((NY, NX * rows, width), f32),
            pltpu.VMEM((NY, NX * rows, width), bf16),
            pltpu.VMEM((NY, rows, width), bf16),
            pltpu.VMEM((NY, rows, width), bf16),
            pltpu.VMEM((NY, rows, width), bf16),
            pltpu.VMEM((NY, rows, width), bf16),
            pltpu.VMEM((rows, width), bf16),
            pltpu.VMEM((rows, width), bf16),
            pltpu.VMEM((rows, width), bf16),
            pltpu.VMEM((NX * rows, width - SPLIT), bf16),
            pltpu.VMEM((NX * rows, width - SPLIT), bf16),
            pltpu.VMEM((NX * rows, width - SPLIT), bf16),
            pltpu.VMEM((rows, width - SPLIT), bf16),
            pltpu.VMEM((rows, width - SPLIT), bf16),
            pltpu.VMEM((rows, width - SPLIT), bf16),
            pltpu.VMEM((NY, NX * rows, units), bf16),
            pltpu.VMEM((N, 1, 128), f32),
            pltpu.VMEM((N, 1, 128), f32),
            pltpu.VMEM((1, 128), f32),
            pltpu.VMEM((N, 1, 128), f32),
            pltpu.SemaphoreType.DMA((8,)),
            pltpu.SemaphoreType.DMA((len(KINDS),)),
            pltpu.SemaphoreType.DMA((ARRIVALS,)),
            pltpu.SemaphoreType.DMA((2, 2)),
        ],
        compiler_params=pltpu.CompilerParams(
            collective_id=0, has_side_effects=True, vmem_limit_bytes=56 * 1024 * 1024
        ),
    )(
        tokens, gate_w, up_w, down_w,
        gain.reshape(1, width), head.reshape(1, width),
        mask.reshape(NX, 128), ids.reshape(NX, 128),
    )
    values, means = pl.pallas_call(
        take_apart,
        out_shape=(jax.ShapeDtypeStruct((1, rows), f32), jax.ShapeDtypeStruct((1, SEQS), f32)),
        in_specs=[pl.BlockSpec(memory_space=pltpu.VMEM)],
        out_specs=(pl.BlockSpec(memory_space=pltpu.VMEM),) * 2,
    )(result)
    return values.reshape(rows), means.reshape(SEQS)


def solution(mesh):
    placed = (
        P(("dp", "tensor"), None),
        P(None, "tensor"),
        P(None, "tensor"),
        P("tensor", None),
        P(),
        P(),
        P("dp"),
        P("dp"),
    )
    return jax.shard_map(
        per_device,
        mesh=mesh,
        in_specs=placed,
        out_specs=(P(("dp", "tensor")), P("dp")),
        check_vma=False,
    )
```

```python
import jax
import jax.numpy as jnp
from jax import lax
from jax.experimental import pallas as pl
from jax.experimental.pallas import tpu as pltpu
from jax.sharding import PartitionSpec as P

SEQS = 16
ROWS = 32
HALF = 16
NX = 4
NY = 4
N = NX * NY
EPS = 1e-06
CHUNK = 512

SPLIT = 1664
ARRIVALS = 64

KIND_ROWS = {"X": 384, "S": 384, "Y": 96, "Z": 96, "XB": 96, "YB": 384, "T": 384, "U": 96}
KINDS = tuple(KIND_ROWS)
GROUPS = {f"{letter}{dy}": 64 for letter in "xs" for dy in range(NY)}
GROUPS.update({"z": 64, "b+": 64, "b-": 64, "bf": 128, "t": 256, "u": 64})

SLOT = (0, 1, 3, 2)

ORDER = [
    "Y:-1 Y:+0 X:0+0 XB:-1",
    "X:0-1 XB:+0 Y:-0 X:0+1",
    "Y:+1 XB:-0 X:0-0 XF:0-",
    "XBF:- XB:+1 XBF:+ XF:0+",
    "YF:- YF:+ X:1-1 YB:0+",
    "X:3-0 X:1+1 YB:1- X:3+0",
    "YB:2+ X:1+0 X:3-1 GU:0",
    "YB:3- XF:1- X:3+1 YB:2-",
    "YB:1+ YB:3+ X:2-1 X:2+0",
    "XF:3- YBF:1 XF:3+ X:2+1",
    "YBF:0 X:2-0 D:0 YBF:2",
    "YBF:3 XF:2- XF:2+ X:1-0",
    "YB:0- XF:1+ GU:3 D:3",
    "S2:3+ S1:3+ S1:3- S2:3-",
    "GU:2 D:2 S2:2+ T2:+",
    "S2:2- T2:- S1:2- GU:1",
    "S1:2+ D:1 S2:1- S2:1+",
    "T1:+ T1:- PA: SF:2+",
    "SF:2- SF:3+ SF:3- TF:+",
    "S1:1- TF:- SF:1- S2:0-",
    "S1:1+ SF:1+ ZA:2 S1:0+",
    "ZA:3 S2:0+ ZA:1 ZB:",
    "S1:0- ZF:1 ZF:3 PB:",
    "SF:0+ SF:0- UF:- UF:+",
    "ZA:0",
]


def kernel(
    tokens, gate_w, up_w, down_w, gain, head, mask, ids,
    values_out, means_out,
    tok, wgu, wd, gain_v, head_v, mask_v, ids_v,
    part, xs, rx2, rxl, rxr, zs, ry2, ryd, ryu, ryb2, rybd, rybu, rxb2, rxbl, rxbr, hidden,
    proj, proj_x, proj_sum, proj_y, line_out, lines,
    local_sem, send_sem, recv_sem, small_sem,
):
    f32, bf16 = jnp.float32, jnp.bfloat16
    me, dp = lax.axis_index("tensor"), lax.axis_index("dp")
    x, y = me // NY, me % NY
    width = tok.shape[2]
    hidden_units = wd.shape[0]

    places_x = [x] + [lax.rem(x + k, NX) for k in range(1, NX)]
    places_y = [y] + [lax.rem(y + k, NY) for k in range(1, NY)]
    device_at = {(dy, dx): places_x[dx] * NY + places_y[dy] for dy in range(NY) for dx in range(NX)}
    right, left, up, down = device_at[0, 1], device_at[0, 3], device_at[1, 0], device_at[3, 0]

    loads = [
        pltpu.make_async_copy(src, dst, local_sem.at[i])
        for i, (src, dst) in enumerate([
            (tokens, tok.at[0, pl.ds(0, ROWS)]),
            (gate_w, wgu.at[:, pl.ds(0, hidden_units)]),
            (up_w, wgu.at[:, pl.ds(hidden_units, hidden_units)]),
            (down_w, wd),
            (gain, gain_v),
            (head, head_v),
            (mask, mask_v),
            (ids, ids_v),
        ])
    ]
    barrier = pltpu.get_barrier_semaphore()
    for other in (right, left, up, down):
        pl.semaphore_signal(
            barrier, inc=1, device_id=(other, dp), device_id_type=pl.DeviceIdType.MESH
        )
    loads[0].start()
    loads[0].wait()
    pl.semaphore_wait(barrier, 4)

    here, weights = set(), []
    arrivals = {}
    first, second = pl.ds(0, SPLIT), pl.ds(SPLIT, width - SPLIT)

    def sized(rows, columns):
        if rows <= NX * ROWS:
            return tok.at[0, pl.ds(0, rows), columns]
        return tok.at[pl.ds(0, rows // (NX * ROWS)), :, columns]

    def await_bytes(like, sem):
        pltpu.make_async_copy(like, like, sem).wait()

    def send(name, src, dst, device, kind, group=None):
        key = group or name
        if key not in arrivals:
            arrivals[key] = (recv_sem.at[len(arrivals)], dst)
        pltpu.make_async_remote_copy(
            src_ref=src, dst_ref=dst, send_sem=send_sem.at[KINDS.index(kind)], recv_sem=arrivals[key][0],
            device_id=(device, dp), device_id_type=pl.DeviceIdType.MESH,
        ).start()

    def arrived(*names):
        for name in names:
            if name not in here:
                sem, dst = arrivals[name]
                if name in GROUPS:
                    dst = sized(GROUPS[name], first if name[0] in "xsz" else second)
                await_bytes(dst, sem)
                here.add(name)

    ring = {"+": (right, up, 3, 0), "-": (left, down, 1, 1)}
    gathered = {dy: set() for dy in range(NY)}

    def rows_of(dx, half):
        return pl.ds(dx * ROWS + half * HALF, HALF)

    def halves(half):
        return pl.ds(half * HALF, HALF)

    y_source = {3: ("Y+0", "Y+1"), 1: ("Y-0", "Y-1"), 2: ("YF+", "YF-")}

    def y_send(d, half):
        src, dst = tok.at[0, rows_of(0, half), first], tok.at[SLOT[ring[d][2]], rows_of(0, half), first]
        send(f"Y{d}{half}", src, dst, ring[d][1], "Y")

    def y_forward(d):
        _, to, dy, half = ring[d]
        arrived(f"Y{d}{half}")
        send(f"YF{d}", tok.at[SLOT[dy], rows_of(0, half), first], tok.at[SLOT[2], rows_of(0, half), first], to, "Y")

    def x_send(dy, d, half):
        if dy:
            arrived(y_source[dy][half])
            gathered[dy].add(y_source[dy][half])
        to, _, dx, ahead = ring[d]
        group = None if half == ahead else f"x{dy}"
        src, dst = tok.at[SLOT[dy], rows_of(0, half), first], tok.at[SLOT[dy], rows_of(dx, half), first]
        send(f"X{dy}{d}{half}", src, dst, to, "X", group)

    def x_forward(dy, d):
        to, _, dx, half = ring[d]
        arrived(f"X{dy}{d}{half}")
        src, dst = tok.at[SLOT[dy], rows_of(dx, half), first], tok.at[SLOT[dy], rows_of(2, half), first]
        send(f"XF{dy}{d}", src, dst, to, "X", f"x{dy}")
        gathered[dy].add(f"x{dy}")

    def xb_send(d, half):
        name = f"XB{d}{half}"
        send(name, tok.at[0, rows_of(0, half), second], tok.at[0, rows_of(ring[d][2], half), second], ring[d][0], "XB")
        gathered[0].add(name)

    def xb_forward(d):
        to, _, dx, half = ring[d]
        arrived(f"XB{d}{half}")
        send(f"XBF{d}", tok.at[0, rows_of(dx, half), second], tok.at[0, rows_of(2, half), second], to, "XB")
        gathered[0].add(f"XBF{d}")

    def yb_send(dx, d):
        arrived(*{0: (), 3: ("XB+0", "XB+1"), 1: ("XB-0", "XB-1"), 2: ("XBF+", "XBF-")}[dx])
        rows = pl.ds(dx * ROWS, ROWS)
        group = None if (dx % 2 == 0) == (d == "+") else f"b{d}"
        send(f"YB{dx}{d}", tok.at[0, rows, second], tok.at[SLOT[ring[d][2]], rows, second], ring[d][1], "YB", group)
        gathered[ring[d][2]].add(group or f"YB{dx}{d}")

    def yb_forward(dx):
        d = "+" if dx % 2 == 0 else "-"
        arrived(f"YB{dx}{d}")
        rows = pl.ds(dx * ROWS, ROWS)
        send(f"YBF{dx}", tok.at[SLOT[ring[d][2]], rows, second], tok.at[SLOT[2], rows, second], ring[d][1], "YB", "bf")
        gathered[2].add("bf")

    lane = lax.broadcasted_iota(jnp.int32, (ROWS, 128), 1)
    row = lax.broadcasted_iota(jnp.int32, (ROWS, 128), 0)
    diagonal = lane % ROWS == row
    def as_line(column):
        return jnp.sum(jnp.where(diagonal, column, 0.0), axis=0, keepdims=True)

    def small_copy(dy, dx, src, dst, pair):
        pltpu.make_async_remote_copy(
            src_ref=src, dst_ref=dst,
            send_sem=small_sem.at[pair, 0], recv_sem=small_sem.at[pair, 1],
            device_id=(device_at[dy, dx], dp), device_id_type=pl.DeviceIdType.MESH,
        ).start()

    def up_project(offsets):
        for dy in offsets:
            arrived(*sorted(gathered[dy]))
        if not weights:
            for load in loads[1:]:
                load.wait()
            weights.append(gain_v[...] * head_v[...])
        at_slot = pl.ds(min(SLOT[dy] for dy in offsets), len(offsets))
        rows = len(offsets) * NX * ROWS
        both = jnp.dot(tok[at_slot].reshape(rows, width), wgu[...], preferred_element_type=f32)
        gate, upper = both[:, :hidden_units], both[:, hidden_units:]
        units = (gate / (1.0 + jnp.exp(-gate)) * upper).astype(bf16)
        hidden[at_slot] = units.reshape(len(offsets), NX * ROWS, hidden_units)

    stay_first = ((0, ROWS + HALF), (4 * ROWS - HALF, 4 * ROWS))
    leave_first = ((ROWS + HALF, 4 * ROWS - HALF),)
    lower_rows, upper_rows = ((0, 2 * ROWS),), ((2 * ROWS, 4 * ROWS),)
    stay_second = {0: ((0, 4 * ROWS),), 1: lower_rows, 2: (), 3: upper_rows}
    leave_second = {0: (), 1: upper_rows, 2: ((0, 4 * ROWS),), 3: lower_rows}

    def down_project(dy):
        units, gv, slot = hidden[SLOT[dy]], weights[0], SLOT[dy]
        lanes = jnp.zeros((NX * ROWS, 128), f32)
        for c in range(0, width, CHUNK):
            terms = jnp.dot(units, wd[:, c:c + CHUNK], preferred_element_type=f32)
            cut = min(max(SPLIT - c, 0), CHUNK)
            for begin, end, stay, leave in (
                (0, cut, stay_first, leave_first), (cut, CHUNK, stay_second[dy], leave_second[dy])
            ):
                if begin == end:
                    continue
                for lo, hi in stay:
                    part[slot, lo:hi, c + begin:c + end] = terms[lo:hi, begin:end]
                for lo, hi in leave:
                    xs[slot, lo:hi, c + begin:c + end] = terms[lo:hi, begin:end].astype(bf16)
            weighted = terms * gv[:, c:c + CHUNK]
            for k in range(0, CHUNK, 128):
                lanes += weighted[:, k:k + 128]
        if dy == 0:
            own = tok[0, :ROWS].astype(f32)
            part[0, :ROWS] = part[0, :ROWS] + own
            weighted = own * gv
            for k in range(0, width, 128):
                own_lanes = weighted[:, k:k + 128] if k == 0 else own_lanes + weighted[:, k:k + 128]
            lanes = jnp.concatenate([lanes[:ROWS] + own_lanes, lanes[ROWS:]], axis=0)
        column = jnp.sum(lanes, axis=1, keepdims=True)
        for dx in range(NX):
            proj[dx, dy] = as_line(column[dx * ROWS:(dx + 1) * ROWS])

    def project_x():
        for dx in range(1, NX):
            small_copy(0, dx, proj.at[dx], proj_x.at[-dx % NX], 0)

    def project_y():
        await_bytes(proj_x.at[pl.ds(1, NX - 1)], small_sem.at[0, 1])
        proj_sum[...] = proj[0] + proj_x[1] + proj_x[2] + proj_x[3]
        for dy in range(1, NY):
            small_copy(dy, 0, proj_sum.at[dy], proj_y.at[-dy % NY], 1)

    def x_sum_far(dy, d):
        half = ring[d][3]
        send(f"S2{dy}{d}", xs.at[SLOT[dy], rows_of(2, half), first], rx2.at[dy, halves(half), first], ring[d][0], "S")

    def x_sum_near(dy, d):
        to, _, back, half = ring[d]
        into = {"+": rxl, "-": rxr}[d]
        src, dst = xs.at[SLOT[dy], rows_of(4 - back, 1 - half), first], into.at[dy, halves(1 - half), first]
        send(f"S1{dy}{d}", src, dst, to, "S", f"s{dy}")

    def x_sum_forward(dy, d):
        to, _, back, half = ring[d]
        arrived(f"S2{dy}{d}")
        into = {"+": rxl, "-": rxr}[d]
        rows = rows_of(4 - back, half)
        xs[SLOT[dy], rows, first] = (part[SLOT[dy], rows, first] + rx2[dy, halves(half), first].astype(f32)).astype(bf16)
        send(f"SF{dy}{d}", xs.at[SLOT[dy], rows, first], into.at[dy, halves(half), first], to, "S", f"s{dy}")

    def x_sum_end(dy):
        arrived(f"s{dy}")
        own = pl.ds(0, ROWS)
        total = part[SLOT[dy], own, first] + rxl[dy, :, first].astype(f32) + rxr[dy, :, first].astype(f32)
        part[SLOT[dy], own, first] = total
        if dy:
            zs[dy, :, first] = total.astype(bf16)
        if dy == 1:
            send("Z1", zs.at[1, halves(1), first], ryd.at[halves(1), first], up, "Z", "z")
        if dy == 3:
            send("Z3", zs.at[3, halves(0), first], ryu.at[halves(0), first], down, "Z", "z")
        if dy == 2:
            send("Z2+", zs.at[2, halves(0), first], ry2.at[halves(0), first], up, "Z")
            send("Z2-", zs.at[2, halves(1), first], ry2.at[halves(1), first], down, "Z")

    def y_sum_forward(dy):
        d, half, into, to = {1: ("+", 0, ryd, up), 3: ("-", 1, ryu, down)}[dy]
        arrived(f"Z2{d}")
        total = part[SLOT[dy], halves(half), first] + ry2[halves(half), first].astype(f32)
        zs[dy, halves(half), first] = total.astype(bf16)
        send(f"Z{dy}F", zs.at[dy, halves(half), first], into.at[halves(half), first], to, "Z", "z")

    lower, upper_half = pl.ds(0, 2 * ROWS), pl.ds(2 * ROWS, 2 * ROWS)

    def yb_sum_far(d):
        rows = {"+": lower, "-": upper_half}[d]
        send(f"T2{d}", xs.at[SLOT[2], rows, second], ryb2.at[rows], ring[d][1], "T")

    def yb_sum_near(d):
        dy, rows, into = {"+": (1, upper_half, rybd), "-": (3, lower, rybu)}[d]
        send(f"T1{d}", xs.at[SLOT[dy], rows, second], into.at[rows], ring[d][1], "T", "t")

    def yb_sum_forward(d):
        arrived(f"T2{d}")
        dy, rows, into = {"+": (1, lower, rybd), "-": (3, upper_half, rybu)}[d]
        xs[SLOT[dy], rows, second] = (part[SLOT[dy], rows, second] + ryb2[rows].astype(f32)).astype(bf16)
        send(f"TF{d}", xs.at[SLOT[dy], rows, second], into.at[rows], ring[d][1], "T", "t")

    def yb_sum_end():
        arrived("t")
        total = part[0, :, second] + rybd[...].astype(f32) + rybu[...].astype(f32)
        part[0, :, second] = total
        xs[0, :, second] = total.astype(bf16)
        for d in "+-":
            to, _, back, half = ring[d]
            into = {"+": rxbl, "-": rxbr}[d]
            send(f"U2{d}", xs.at[0, rows_of(2, half), second], rxb2.at[halves(half)], to, "U")
            send(f"U1{d}", xs.at[0, rows_of(4 - back, 1 - half), second], into.at[halves(1 - half)], to, "U", "u")

    def xb_sum_forward(d):
        to, _, back, half = ring[d]
        arrived(f"U2{d}")
        into = {"+": rxbl, "-": rxbr}[d]
        rows = rows_of(4 - back, half)
        xs[0, rows, second] = (part[0, rows, second] + rxb2[halves(half)].astype(f32)).astype(bf16)
        send(f"UF{d}", xs.at[0, rows, second], into.at[halves(half)], to, "U", "u")

    steps = {
        "Y": lambda k: y_send(k[0], int(k[1])),
        "YF": y_forward,
        "X": lambda k: x_send(int(k[0]), k[1], int(k[2])),
        "XF": lambda k: x_forward(int(k[0]), k[1]),
        "XB": lambda k: xb_send(k[0], int(k[1])),
        "XBF": xb_forward,
        "YB": lambda k: yb_send(int(k[0]), k[1]),
        "YBF": lambda k: yb_forward(int(k)),
        "GU": lambda k: up_project([int(q) for q in k]),
        "D": lambda k: down_project(int(k)),
        "PA": lambda k: project_x(),
        "PB": lambda k: project_y(),
        "S2": lambda k: x_sum_far(int(k[0]), k[1]),
        "S1": lambda k: x_sum_near(int(k[0]), k[1]),
        "SF": lambda k: x_sum_forward(int(k[0]), k[1]),
        "ZA": lambda k: x_sum_end(int(k)),
        "ZF": lambda k: y_sum_forward(int(k)),
        "T2": yb_sum_far,
        "T1": yb_sum_near,
        "TF": yb_sum_forward,
        "ZB": lambda k: yb_sum_end(),
        "UF": xb_sum_forward,
    }
    for number, line in enumerate(ORDER):
        if number == 2:
            for load in loads[1:]:
                load.start()
        for step in line.split():
            kind, _, key = step.partition(":")
            steps[kind](key)

    mask_f = mask_v[...].astype(f32)
    sequence = lax.broadcasted_iota(jnp.int32, (SEQS, 128), 0)
    chosen = [
        jnp.where(ids_v[r:r + 1, :] == sequence, mask_f[r:r + 1, :], 0.0) for r in range(NX)
    ]
    counts = jnp.sum(chosen[0] + chosen[1] + chosen[2] + chosen[3], axis=1, keepdims=True)

    others = pl.ds(1, N - 1)
    await_bytes(proj_y.at[pl.ds(1, NY - 1)], small_sem.at[1, 1])
    projected = proj_sum[0] + proj_y[1] + proj_y[2] + proj_y[3]
    own = pl.ds(0, ROWS)
    arrived("z")
    block = part[0, own, first] + ryd[:, first].astype(f32) + ryu[:, first].astype(f32)
    total = jnp.sum(block * block, axis=1, keepdims=True)
    arrived("u")
    block = part[0, own, second] + rxbl[...].astype(f32) + rxbr[...].astype(f32)
    total += jnp.sum(block * block, axis=1, keepdims=True)
    line = projected * lax.rsqrt(as_line(total) / width + EPS)
    mine = jnp.where(lax.broadcasted_iota(jnp.int32, (1, 128), 1) // ROWS == y, line, 0.0)
    line_out[...] = mine
    lines[0] = mine
    far_first = sorted(
        ((dy, dx) for dy in range(NY) for dx in range(NX) if dy or dx),
        key=lambda q: -2 * min(q[0], NY - q[0]) - min(q[1], NX - q[1]),
    )
    for dy, dx in far_first:
        small_copy(dy, dx, line_out, lines.at[-dy % NY * NX + -dx % NX], 2)
    for kind, rows in KIND_ROWS.items():
        await_bytes(sized(rows, first if kind in ("X", "S", "Y", "Z") else second), send_sem.at[KINDS.index(kind)])
    await_bytes(proj_x.at[pl.ds(1, NX - 1)], small_sem.at[0, 0])
    await_bytes(proj_y.at[pl.ds(1, NY - 1)], small_sem.at[1, 0])
    await_bytes(lines.at[others], small_sem.at[2, 1])
    tile_row = lax.broadcasted_iota(jnp.int32, (8, 128), 0)
    values = jnp.zeros((8, 128), f32)
    for dx in range(NX):
        column = lines[dx] + lines[NX + dx] + lines[2 * NX + dx] + lines[3 * NX + dx]
        values += jnp.where(tile_row == places_x[dx], column, 0.0)
    sums = chosen[0] * values[0:1]
    for r in range(1, NX):
        sums += chosen[r] * values[r:r + 1]
    means = jnp.sum(sums, axis=1, keepdims=True) / jnp.maximum(counts, 1.0)
    place = lax.broadcasted_iota(jnp.int32, (SEQS, 128), 1)
    means_out[...] = jnp.sum(jnp.where(place == sequence, means, 0.0), axis=0, keepdims=True)[:, :SEQS]
    values_out[...] = line[:, :ROWS]
    await_bytes(lines.at[others], small_sem.at[2, 0])


def per_device(tokens, gate_w, up_w, down_w, gain, head, mask, ids):
    rows, width = tokens.shape
    units = gate_w.shape[1]
    bf16, f32 = jnp.bfloat16, jnp.float32
    anywhere = pl.BlockSpec(memory_space=pl.ANY)
    values, means = pl.pallas_call(
        kernel,
        out_shape=(pltpu.VMEM((1, rows), f32), pltpu.VMEM((1, SEQS), f32)),
        in_specs=[anywhere] * 8,
        out_specs=(pl.BlockSpec(memory_space=pltpu.VMEM),) * 2,
        scratch_shapes=[
            pltpu.VMEM((NY, NX * rows, width), bf16),
            pltpu.VMEM((width, 2 * units), bf16),
            pltpu.VMEM((units, width), bf16),
            pltpu.VMEM((1, width), f32),
            pltpu.VMEM((1, width), f32),
            pltpu.VMEM((NX, 128), jnp.int32),
            pltpu.VMEM((NX, 128), jnp.int32),
            pltpu.VMEM((NY, NX * rows, width), f32),
            pltpu.VMEM((NY, NX * rows, width), bf16),
            pltpu.VMEM((NY, rows, width), bf16),
            pltpu.VMEM((NY, rows, width), bf16),
            pltpu.VMEM((NY, rows, width), bf16),
            pltpu.VMEM((NY, rows, width), bf16),
            pltpu.VMEM((rows, width), bf16),
            pltpu.VMEM((rows, width), bf16),
            pltpu.VMEM((rows, width), bf16),
            pltpu.VMEM((NX * rows, width - SPLIT), bf16),
            pltpu.VMEM((NX * rows, width - SPLIT), bf16),
            pltpu.VMEM((NX * rows, width - SPLIT), bf16),
            pltpu.VMEM((rows, width - SPLIT), bf16),
            pltpu.VMEM((rows, width - SPLIT), bf16),
            pltpu.VMEM((rows, width - SPLIT), bf16),
            pltpu.VMEM((NY, NX * rows, units), bf16),
            pltpu.VMEM((NX, NY, 1, 128), f32),
            pltpu.VMEM((NX, NY, 1, 128), f32),
            pltpu.VMEM((NY, 1, 128), f32),
            pltpu.VMEM((NY, 1, 128), f32),
            pltpu.VMEM((1, 128), f32),
            pltpu.VMEM((N, 1, 128), f32),
            pltpu.SemaphoreType.DMA((8,)),
            pltpu.SemaphoreType.DMA((len(KINDS),)),
            pltpu.SemaphoreType.DMA((ARRIVALS,)),
            pltpu.SemaphoreType.DMA((3, 2)),
        ],
        compiler_params=pltpu.CompilerParams(
            collective_id=0, has_side_effects=True, vmem_limit_bytes=56 * 1024 * 1024
        ),
    )(
        tokens, gate_w, up_w, down_w,
        gain.reshape(1, width), head.reshape(1, width),
        mask.reshape(NX, 128), ids.reshape(NX, 128),
    )
    return values.reshape(rows), means.reshape(SEQS)


def solution(mesh):
    placed = (
        P(("dp", "tensor"), None),
        P(None, "tensor"),
        P(None, "tensor"),
        P("tensor", None),
        P(),
        P(),
        P("dp"),
        P("dp"),
    )
    return jax.shard_map(
        per_device,
        mesh=mesh,
        in_specs=placed,
        out_specs=(P(("dp", "tensor")), P("dp")),
        check_vma=False,
    )
```

```python
import jax
import jax.numpy as jnp
from jax import lax
from jax.experimental import pallas as pl
from jax.experimental.pallas import tpu as pltpu
from jax.sharding import PartitionSpec as P

SEQS = 16
ROWS = 32
HALF = 16
NX = 4
NY = 4
N = NX * NY
EPS = 1e-06
CHUNK = 512

SPLIT = 1664
ARRIVALS = 64

KIND_ROWS = {"X": 384, "S": 384, "Y": 96, "Z": 96, "XB": 96, "YB": 384, "T": 384, "U": 96}
KINDS = tuple(KIND_ROWS)
GROUPS = {f"{letter}{dy}": 64 for letter in "xs" for dy in range(NY)}
GROUPS.update({"z": 64, "b+": 64, "b-": 64, "bf": 128, "t": 256, "u": 64})

SLOT = (0, 1, 3, 2)

ORDER = [
    "Y:-1 Y:+0 X:0+0 XB:-1",
    "X:0-1 XB:+0 Y:-0 X:0+1",
    "Y:+1 XB:-0 X:0-0 XF:0-",
    "XBF:- XB:+1 XBF:+ XF:0+",
    "YF:- YF:+ X:1-1 YB:0+",
    "X:3-0 X:1+1 YB:1- X:3+0",
    "YB:2+ X:1+0 X:3-1 GU:0",
    "YB:3- XF:1- X:3+1 YB:2-",
    "YB:1+ YB:3+ X:2-1 X:2+0",
    "XF:3- YBF:1 XF:3+ X:2+1",
    "YBF:0 X:2-0 D:0 YBF:2",
    "YBF:3 XF:2- XF:2+ X:1-0",
    "YB:0- XF:1+ GU:3 D:3",
    "S2:3+ S1:3+ S1:3- S2:3-",
    "GU:2 D:2 S2:2+ T2:+",
    "S2:2- T2:- S1:2- GU:1",
    "S1:2+ D:1 S2:1- S2:1+",
    "T1:+ T1:- PA: SF:2+",
    "SF:2- SF:3+ SF:3- TF:+",
    "S1:1- TF:- SF:1- S2:0-",
    "S1:1+ SF:1+ ZA:2 S1:0+",
    "ZA:3 S2:0+ ZA:1 ZB:",
    "S1:0- ZF:1 ZF:3 PB:",
    "SF:0+ SF:0- UF:- UF:+",
    "ZA:0",
]


def kernel(
    tokens, gate_w, up_w, down_w, gain, head, mask, ids,
    values_out, means_out,
    tok, wgu, wd, gain_v, head_v, mask_v, ids_v,
    part, xs, rx2, rxl, rxr, zs, ry2, ryd, ryu, ryb2, rybd, rybu, rxb2, rxbl, rxbr, hidden,
    proj, proj_x, proj_sum, proj_y, line_out, lines,
    local_sem, send_sem, recv_sem, small_sem,
):
    f32, bf16 = jnp.float32, jnp.bfloat16
    me, dp = lax.axis_index("tensor"), lax.axis_index("dp")
    x, y = me // NY, me % NY
    width = tok.shape[2]
    hidden_units = wd.shape[0]

    places_x = [x] + [lax.rem(x + k, NX) for k in range(1, NX)]
    places_y = [y] + [lax.rem(y + k, NY) for k in range(1, NY)]
    device_at = {(dy, dx): places_x[dx] * NY + places_y[dy] for dy in range(NY) for dx in range(NX)}
    right, left, up, down = device_at[0, 1], device_at[0, 3], device_at[1, 0], device_at[3, 0]

    loads = [
        pltpu.make_async_copy(src, dst, local_sem.at[i])
        for i, (src, dst) in enumerate([
            (tokens, tok.at[0, pl.ds(0, ROWS)]),
            (gate_w, wgu.at[:, pl.ds(0, hidden_units)]),
            (up_w, wgu.at[:, pl.ds(hidden_units, hidden_units)]),
            (down_w, wd),
            (gain, gain_v),
            (head, head_v),
            (mask, mask_v),
            (ids, ids_v),
        ])
    ]
    barrier = pltpu.get_barrier_semaphore()
    for other in (right, left, up, down):
        pl.semaphore_signal(
            barrier, inc=1, device_id=(other, dp), device_id_type=pl.DeviceIdType.MESH
        )
    loads[0].start()

    is_odd = lax.rem(dp, 2) == 1

    @pl.when(is_odd)
    def _():
        for load in loads[1:]:
            load.start()
        for load in loads[1:]:
            load.wait()

    loads[0].wait()
    pl.semaphore_wait(barrier, 4)

    here, weights = set(), []
    arrivals = {}
    first, second = pl.ds(0, SPLIT), pl.ds(SPLIT, width - SPLIT)

    def sized(rows, columns):
        if rows <= NX * ROWS:
            return tok.at[0, pl.ds(0, rows), columns]
        return tok.at[pl.ds(0, rows // (NX * ROWS)), :, columns]

    def await_bytes(like, sem):
        pltpu.make_async_copy(like, like, sem).wait()

    def send(name, src, dst, device, kind, group=None):
        key = group or name
        if key not in arrivals:
            arrivals[key] = (recv_sem.at[len(arrivals)], dst)
        pltpu.make_async_remote_copy(
            src_ref=src, dst_ref=dst, send_sem=send_sem.at[KINDS.index(kind)], recv_sem=arrivals[key][0],
            device_id=(device, dp), device_id_type=pl.DeviceIdType.MESH,
        ).start()

    def arrived(*names):
        for name in names:
            if name not in here:
                sem, dst = arrivals[name]
                if name in GROUPS:
                    dst = sized(GROUPS[name], first if name[0] in "xsz" else second)
                await_bytes(dst, sem)
                here.add(name)

    ring = {"+": (right, up, 3, 0), "-": (left, down, 1, 1)}
    gathered = {dy: set() for dy in range(NY)}

    def rows_of(dx, half):
        return pl.ds(dx * ROWS + half * HALF, HALF)

    def halves(half):
        return pl.ds(half * HALF, HALF)

    y_source = {3: ("Y+0", "Y+1"), 1: ("Y-0", "Y-1"), 2: ("YF+", "YF-")}

    def y_send(d, half):
        src, dst = tok.at[0, rows_of(0, half), first], tok.at[SLOT[ring[d][2]], rows_of(0, half), first]
        send(f"Y{d}{half}", src, dst, ring[d][1], "Y")

    def y_forward(d):
        _, to, dy, half = ring[d]
        arrived(f"Y{d}{half}")
        send(f"YF{d}", tok.at[SLOT[dy], rows_of(0, half), first], tok.at[SLOT[2], rows_of(0, half), first], to, "Y")

    def x_send(dy, d, half):
        if dy:
            arrived(y_source[dy][half])
            gathered[dy].add(y_source[dy][half])
        to, _, dx, ahead = ring[d]
        group = None if half == ahead else f"x{dy}"
        src, dst = tok.at[SLOT[dy], rows_of(0, half), first], tok.at[SLOT[dy], rows_of(dx, half), first]
        send(f"X{dy}{d}{half}", src, dst, to, "X", group)

    def x_forward(dy, d):
        to, _, dx, half = ring[d]
        arrived(f"X{dy}{d}{half}")
        src, dst = tok.at[SLOT[dy], rows_of(dx, half), first], tok.at[SLOT[dy], rows_of(2, half), first]
        send(f"XF{dy}{d}", src, dst, to, "X", f"x{dy}")
        gathered[dy].add(f"x{dy}")

    def xb_send(d, half):
        name = f"XB{d}{half}"
        send(name, tok.at[0, rows_of(0, half), second], tok.at[0, rows_of(ring[d][2], half), second], ring[d][0], "XB")
        gathered[0].add(name)

    def xb_forward(d):
        to, _, dx, half = ring[d]
        arrived(f"XB{d}{half}")
        send(f"XBF{d}", tok.at[0, rows_of(dx, half), second], tok.at[0, rows_of(2, half), second], to, "XB")
        gathered[0].add(f"XBF{d}")

    def yb_send(dx, d):
        arrived(*{0: (), 3: ("XB+0", "XB+1"), 1: ("XB-0", "XB-1"), 2: ("XBF+", "XBF-")}[dx])
        rows = pl.ds(dx * ROWS, ROWS)
        group = None if (dx % 2 == 0) == (d == "+") else f"b{d}"
        send(f"YB{dx}{d}", tok.at[0, rows, second], tok.at[SLOT[ring[d][2]], rows, second], ring[d][1], "YB", group)
        gathered[ring[d][2]].add(group or f"YB{dx}{d}")

    def yb_forward(dx):
        d = "+" if dx % 2 == 0 else "-"
        arrived(f"YB{dx}{d}")
        rows = pl.ds(dx * ROWS, ROWS)
        send(f"YBF{dx}", tok.at[SLOT[ring[d][2]], rows, second], tok.at[SLOT[2], rows, second], ring[d][1], "YB", "bf")
        gathered[2].add("bf")

    lane = lax.broadcasted_iota(jnp.int32, (ROWS, 128), 1)
    row = lax.broadcasted_iota(jnp.int32, (ROWS, 128), 0)
    diagonal = lane % ROWS == row
    def as_line(column):
        return jnp.sum(jnp.where(diagonal, column, 0.0), axis=0, keepdims=True)

    def small_copy(dy, dx, src, dst, pair):
        pltpu.make_async_remote_copy(
            src_ref=src, dst_ref=dst,
            send_sem=small_sem.at[pair, 0], recv_sem=small_sem.at[pair, 1],
            device_id=(device_at[dy, dx], dp), device_id_type=pl.DeviceIdType.MESH,
        ).start()

    def up_project(offsets):
        for dy in offsets:
            arrived(*sorted(gathered[dy]))
        if not weights:

            @pl.when(jnp.logical_not(is_odd))
            def _():
                for load in loads[1:]:
                    load.wait()

            weights.append(gain_v[...] * head_v[...])
        at_slot = pl.ds(min(SLOT[dy] for dy in offsets), len(offsets))
        rows = len(offsets) * NX * ROWS
        both = jnp.dot(tok[at_slot].reshape(rows, width), wgu[...], preferred_element_type=f32)
        gate, upper = both[:, :hidden_units], both[:, hidden_units:]
        units = (gate / (1.0 + jnp.exp(-gate)) * upper).astype(bf16)
        hidden[at_slot] = units.reshape(len(offsets), NX * ROWS, hidden_units)

    stay_first = ((0, ROWS + HALF), (4 * ROWS - HALF, 4 * ROWS))
    leave_first = ((ROWS + HALF, 4 * ROWS - HALF),)
    lower_rows, upper_rows = ((0, 2 * ROWS),), ((2 * ROWS, 4 * ROWS),)
    stay_second = {0: ((0, 4 * ROWS),), 1: lower_rows, 2: (), 3: upper_rows}
    leave_second = {0: (), 1: upper_rows, 2: ((0, 4 * ROWS),), 3: lower_rows}

    def down_project(dy):
        units, gv, slot = hidden[SLOT[dy]], weights[0], SLOT[dy]
        lanes = jnp.zeros((NX * ROWS, 128), f32)
        for c in range(0, width, CHUNK):
            terms = jnp.dot(units, wd[:, c:c + CHUNK], preferred_element_type=f32)
            cut = min(max(SPLIT - c, 0), CHUNK)
            for begin, end, stay, leave in (
                (0, cut, stay_first, leave_first), (cut, CHUNK, stay_second[dy], leave_second[dy])
            ):
                if begin == end:
                    continue
                for lo, hi in stay:
                    part[slot, lo:hi, c + begin:c + end] = terms[lo:hi, begin:end]
                for lo, hi in leave:
                    xs[slot, lo:hi, c + begin:c + end] = terms[lo:hi, begin:end].astype(bf16)
            weighted = terms * gv[:, c:c + CHUNK]
            for k in range(0, CHUNK, 128):
                lanes += weighted[:, k:k + 128]
        if dy == 0:
            own = tok[0, :ROWS].astype(f32)
            part[0, :ROWS] = part[0, :ROWS] + own
            weighted = own * gv
            for k in range(0, width, 128):
                own_lanes = weighted[:, k:k + 128] if k == 0 else own_lanes + weighted[:, k:k + 128]
            lanes = jnp.concatenate([lanes[:ROWS] + own_lanes, lanes[ROWS:]], axis=0)
        column = jnp.sum(lanes, axis=1, keepdims=True)
        for dx in range(NX):
            proj[dx, dy] = as_line(column[dx * ROWS:(dx + 1) * ROWS])

    def project_x():
        for dx in range(1, NX):
            small_copy(0, dx, proj.at[dx], proj_x.at[-dx % NX], 0)

    def project_y():
        await_bytes(proj_x.at[pl.ds(1, NX - 1)], small_sem.at[0, 1])
        proj_sum[...] = proj[0] + proj_x[1] + proj_x[2] + proj_x[3]
        for dy in range(1, NY):
            small_copy(dy, 0, proj_sum.at[dy], proj_y.at[-dy % NY], 1)

    def x_sum_far(dy, d):
        half = ring[d][3]
        send(f"S2{dy}{d}", xs.at[SLOT[dy], rows_of(2, half), first], rx2.at[dy, halves(half), first], ring[d][0], "S")

    def x_sum_near(dy, d):
        to, _, back, half = ring[d]
        into = {"+": rxl, "-": rxr}[d]
        src, dst = xs.at[SLOT[dy], rows_of(4 - back, 1 - half), first], into.at[dy, halves(1 - half), first]
        send(f"S1{dy}{d}", src, dst, to, "S", f"s{dy}")

    def x_sum_forward(dy, d):
        to, _, back, half = ring[d]
        arrived(f"S2{dy}{d}")
        into = {"+": rxl, "-": rxr}[d]
        rows = rows_of(4 - back, half)
        xs[SLOT[dy], rows, first] = (part[SLOT[dy], rows, first] + rx2[dy, halves(half), first].astype(f32)).astype(bf16)
        send(f"SF{dy}{d}", xs.at[SLOT[dy], rows, first], into.at[dy, halves(half), first], to, "S", f"s{dy}")

    def x_sum_end(dy):
        arrived(f"s{dy}")
        own = pl.ds(0, ROWS)
        total = part[SLOT[dy], own, first] + rxl[dy, :, first].astype(f32) + rxr[dy, :, first].astype(f32)
        part[SLOT[dy], own, first] = total
        if dy:
            zs[dy, :, first] = total.astype(bf16)
        if dy == 1:
            send("Z1", zs.at[1, halves(1), first], ryd.at[halves(1), first], up, "Z", "z")
        if dy == 3:
            send("Z3", zs.at[3, halves(0), first], ryu.at[halves(0), first], down, "Z", "z")
        if dy == 2:
            send("Z2+", zs.at[2, halves(0), first], ry2.at[halves(0), first], up, "Z")
            send("Z2-", zs.at[2, halves(1), first], ry2.at[halves(1), first], down, "Z")

    def y_sum_forward(dy):
        d, half, into, to = {1: ("+", 0, ryd, up), 3: ("-", 1, ryu, down)}[dy]
        arrived(f"Z2{d}")
        total = part[SLOT[dy], halves(half), first] + ry2[halves(half), first].astype(f32)
        zs[dy, halves(half), first] = total.astype(bf16)
        send(f"Z{dy}F", zs.at[dy, halves(half), first], into.at[halves(half), first], to, "Z", "z")

    lower, upper_half = pl.ds(0, 2 * ROWS), pl.ds(2 * ROWS, 2 * ROWS)

    def yb_sum_far(d):
        rows = {"+": lower, "-": upper_half}[d]
        send(f"T2{d}", xs.at[SLOT[2], rows, second], ryb2.at[rows], ring[d][1], "T")

    def yb_sum_near(d):
        dy, rows, into = {"+": (1, upper_half, rybd), "-": (3, lower, rybu)}[d]
        send(f"T1{d}", xs.at[SLOT[dy], rows, second], into.at[rows], ring[d][1], "T", "t")

    def yb_sum_forward(d):
        arrived(f"T2{d}")
        dy, rows, into = {"+": (1, lower, rybd), "-": (3, upper_half, rybu)}[d]
        xs[SLOT[dy], rows, second] = (part[SLOT[dy], rows, second] + ryb2[rows].astype(f32)).astype(bf16)
        send(f"TF{d}", xs.at[SLOT[dy], rows, second], into.at[rows], ring[d][1], "T", "t")

    def yb_sum_end():
        arrived("t")
        total = part[0, :, second] + rybd[...].astype(f32) + rybu[...].astype(f32)
        part[0, :, second] = total
        xs[0, :, second] = total.astype(bf16)
        for d in "+-":
            to, _, back, half = ring[d]
            into = {"+": rxbl, "-": rxbr}[d]
            send(f"U2{d}", xs.at[0, rows_of(2, half), second], rxb2.at[halves(half)], to, "U")
            send(f"U1{d}", xs.at[0, rows_of(4 - back, 1 - half), second], into.at[halves(1 - half)], to, "U", "u")

    def xb_sum_forward(d):
        to, _, back, half = ring[d]
        arrived(f"U2{d}")
        into = {"+": rxbl, "-": rxbr}[d]
        rows = rows_of(4 - back, half)
        xs[0, rows, second] = (part[0, rows, second] + rxb2[halves(half)].astype(f32)).astype(bf16)
        send(f"UF{d}", xs.at[0, rows, second], into.at[halves(half)], to, "U", "u")

    steps = {
        "Y": lambda k: y_send(k[0], int(k[1])),
        "YF": y_forward,
        "X": lambda k: x_send(int(k[0]), k[1], int(k[2])),
        "XF": lambda k: x_forward(int(k[0]), k[1]),
        "XB": lambda k: xb_send(k[0], int(k[1])),
        "XBF": xb_forward,
        "YB": lambda k: yb_send(int(k[0]), k[1]),
        "YBF": lambda k: yb_forward(int(k)),
        "GU": lambda k: up_project([int(q) for q in k]),
        "D": lambda k: down_project(int(k)),
        "PA": lambda k: project_x(),
        "PB": lambda k: project_y(),
        "S2": lambda k: x_sum_far(int(k[0]), k[1]),
        "S1": lambda k: x_sum_near(int(k[0]), k[1]),
        "SF": lambda k: x_sum_forward(int(k[0]), k[1]),
        "ZA": lambda k: x_sum_end(int(k)),
        "ZF": lambda k: y_sum_forward(int(k)),
        "T2": yb_sum_far,
        "T1": yb_sum_near,
        "TF": yb_sum_forward,
        "ZB": lambda k: yb_sum_end(),
        "UF": xb_sum_forward,
    }
    for number, line in enumerate(ORDER):
        if number == 2:

            @pl.when(jnp.logical_not(is_odd))
            def _():
                for load in loads[1:]:
                    load.start()

        for step in line.split():
            kind, _, key = step.partition(":")
            steps[kind](key)

    mask_f = mask_v[...].astype(f32)
    sequence = lax.broadcasted_iota(jnp.int32, (SEQS, 128), 0)
    chosen = [
        jnp.where(ids_v[r:r + 1, :] == sequence, mask_f[r:r + 1, :], 0.0) for r in range(NX)
    ]
    counts = jnp.sum(chosen[0] + chosen[1] + chosen[2] + chosen[3], axis=1, keepdims=True)

    others = pl.ds(1, N - 1)
    await_bytes(proj_y.at[pl.ds(1, NY - 1)], small_sem.at[1, 1])
    projected = proj_sum[0] + proj_y[1] + proj_y[2] + proj_y[3]
    own = pl.ds(0, ROWS)
    arrived("z")
    block = part[0, own, first] + ryd[:, first].astype(f32) + ryu[:, first].astype(f32)
    total = jnp.sum(block * block, axis=1, keepdims=True)
    arrived("u")
    block = part[0, own, second] + rxbl[...].astype(f32) + rxbr[...].astype(f32)
    total += jnp.sum(block * block, axis=1, keepdims=True)
    line = projected * lax.rsqrt(as_line(total) / width + EPS)
    mine = jnp.where(lax.broadcasted_iota(jnp.int32, (1, 128), 1) // ROWS == y, line, 0.0)
    line_out[...] = mine
    lines[0] = mine
    far_first = sorted(
        ((dy, dx) for dy in range(NY) for dx in range(NX) if dy or dx),
        key=lambda q: -2 * min(q[0], NY - q[0]) - min(q[1], NX - q[1]),
    )
    for dy, dx in far_first:
        small_copy(dy, dx, line_out, lines.at[-dy % NY * NX + -dx % NX], 2)
    for kind, rows in KIND_ROWS.items():
        await_bytes(sized(rows, first if kind in ("X", "S", "Y", "Z") else second), send_sem.at[KINDS.index(kind)])
    await_bytes(proj_x.at[pl.ds(1, NX - 1)], small_sem.at[0, 0])
    await_bytes(proj_y.at[pl.ds(1, NY - 1)], small_sem.at[1, 0])
    await_bytes(lines.at[others], small_sem.at[2, 1])
    tile_row = lax.broadcasted_iota(jnp.int32, (8, 128), 0)
    values = jnp.zeros((8, 128), f32)
    for dx in range(NX):
        column = lines[dx] + lines[NX + dx] + lines[2 * NX + dx] + lines[3 * NX + dx]
        values += jnp.where(tile_row == places_x[dx], column, 0.0)
    sums = chosen[0] * values[0:1]
    for r in range(1, NX):
        sums += chosen[r] * values[r:r + 1]
    means = jnp.sum(sums, axis=1, keepdims=True) / jnp.maximum(counts, 1.0)
    place = lax.broadcasted_iota(jnp.int32, (SEQS, 128), 1)
    means_out[...] = jnp.sum(jnp.where(place == sequence, means, 0.0), axis=0, keepdims=True)[:, :SEQS]
    values_out[...] = line[:, :ROWS]
    await_bytes(lines.at[others], small_sem.at[2, 0])


def per_device(tokens, gate_w, up_w, down_w, gain, head, mask, ids):
    rows, width = tokens.shape
    units = gate_w.shape[1]
    bf16, f32 = jnp.bfloat16, jnp.float32
    anywhere = pl.BlockSpec(memory_space=pl.ANY)
    values, means = pl.pallas_call(
        kernel,
        out_shape=(pltpu.VMEM((1, rows), f32), pltpu.VMEM((1, SEQS), f32)),
        in_specs=[anywhere] * 8,
        out_specs=(pl.BlockSpec(memory_space=pltpu.VMEM),) * 2,
        scratch_shapes=[
            pltpu.VMEM((NY, NX * rows, width), bf16),
            pltpu.VMEM((width, 2 * units), bf16),
            pltpu.VMEM((units, width), bf16),
            pltpu.VMEM((1, width), f32),
            pltpu.VMEM((1, width), f32),
            pltpu.VMEM((NX, 128), jnp.int32),
            pltpu.VMEM((NX, 128), jnp.int32),
            pltpu.VMEM((NY, NX * rows, width), f32),
            pltpu.VMEM((NY, NX * rows, width), bf16),
            pltpu.VMEM((NY, rows, width), bf16),
            pltpu.VMEM((NY, rows, width), bf16),
            pltpu.VMEM((NY, rows, width), bf16),
            pltpu.VMEM((NY, rows, width), bf16),
            pltpu.VMEM((rows, width), bf16),
            pltpu.VMEM((rows, width), bf16),
            pltpu.VMEM((rows, width), bf16),
            pltpu.VMEM((NX * rows, width - SPLIT), bf16),
            pltpu.VMEM((NX * rows, width - SPLIT), bf16),
            pltpu.VMEM((NX * rows, width - SPLIT), bf16),
            pltpu.VMEM((rows, width - SPLIT), bf16),
            pltpu.VMEM((rows, width - SPLIT), bf16),
            pltpu.VMEM((rows, width - SPLIT), bf16),
            pltpu.VMEM((NY, NX * rows, units), bf16),
            pltpu.VMEM((NX, NY, 1, 128), f32),
            pltpu.VMEM((NX, NY, 1, 128), f32),
            pltpu.VMEM((NY, 1, 128), f32),
            pltpu.VMEM((NY, 1, 128), f32),
            pltpu.VMEM((1, 128), f32),
            pltpu.VMEM((N, 1, 128), f32),
            pltpu.SemaphoreType.DMA((8,)),
            pltpu.SemaphoreType.DMA((len(KINDS),)),
            pltpu.SemaphoreType.DMA((ARRIVALS,)),
            pltpu.SemaphoreType.DMA((3, 2)),
        ],
        compiler_params=pltpu.CompilerParams(
            collective_id=0, has_side_effects=True, vmem_limit_bytes=56 * 1024 * 1024
        ),
    )(
        tokens, gate_w, up_w, down_w,
        gain.reshape(1, width), head.reshape(1, width),
        mask.reshape(NX, 128), ids.reshape(NX, 128),
    )
    return values.reshape(rows), means.reshape(SEQS)


def solution(mesh):
    placed = (
        P(("dp", "tensor"), None),
        P(None, "tensor"),
        P(None, "tensor"),
        P("tensor", None),
        P(),
        P(),
        P("dp"),
        P("dp"),
    )
    return jax.shard_map(
        per_device,
        mesh=mesh,
        in_specs=placed,
        out_specs=(P(("dp", "tensor")), P("dp")),
        check_vma=False,
    )
```
